512 devices in a mesh: seq: 32 (over x, y, core), head: 16 (over z).
Axes of the slice: x: 4, y: 4, z: 16, core: 2. Of those that a mesh axis runs over, the one named last changes fastest.
Arguments:
- queries: bfloat16 [4096, 8192], P('seq', 'head'), may hold values from -6 to 6
- keys: bfloat16 [4096, 1024], P('seq'), may hold values from -6 to 6
- values: bfloat16 [4096, 1024], P('seq'), may hold values from -6 to 6
- doc_lengths: int32 [12], replicated, may hold values from 1 to 2048, 4096 in all
- fq_weight: bfloat16 [64, 128, 128], P('head'), may hold values from -1 to 1
- fk_weight: bfloat16 [64, 128, 128], P('head'), may hold values from -1 to 1
Outputs:
- residual: float32 [4096, 8192], P('seq', 'head')
- token_loss: float32 [4096], P('seq')
The draws below stay inside these ranges and needn't reach their ends.
Inputs may be any that keep to these rules, and one draw needn't show every extreme that they name: `doc_lengths`: the 12 documents are packed in order and their lengths sum to 4096; the longest has exactly 2048 tokens.
All inputs are finite; a program needn't handle non-finite values.
Results may differ from the reference program's by a relative error of at most 0.0035.
Values may be sent and summed in bfloat16 or wider, within the bound.
No kernel may reach another device: no remote copies, remote signals or barrier semaphores. Data moves between devices by JAX's collectives and lax.ppermute only.
A program may use at most 64 MiB of HBM per device.

```python
import math
import jax
import jax.numpy as jnp
import numpy as np
from jax import lax

QH = 64
KVH = 8
HD = 128
FH = 128
DOCS = 12
TOKENS = 4096
MAXDOC = 2048


def drawn_rows(key, shape):
    return jnp.clip(jax.random.normal(key, shape, jnp.float32), -6.0, 6.0)


def drawn_weight(key, salt):
    bound = min(6.0 * HD ** (-0.5), 1.0)
    drawn = jax.random.normal(jax.random.fold_in(key, salt), (QH, HD, FH), jnp.float32) * HD ** (-0.5)
    return jnp.clip(drawn, -bound, bound)


def draw_queries(key, part):
    result = drawn_rows(key, (TOKENS, QH * HD))
    return result.astype(jnp.bfloat16)


def draw_keys(key, part):
    own_key = jax.random.fold_in(key, 31)
    result = drawn_rows(own_key, (TOKENS, KVH * HD))
    return result.astype(jnp.bfloat16)


def draw_fq_weight(key, part):
    result = drawn_weight(key, 41)
    return result.astype(jnp.bfloat16)


def draw_fk_weight(key, part):
    result = drawn_weight(key, 51)
    return result.astype(jnp.bfloat16)


def steps_of(key, shape, pieces, low, high):
    def one(axis_at, blocks):
        heights = jax.random.uniform(jax.random.fold_in(jax.random.fold_in(key, 6), axis_at), (blocks,), jnp.float32, low / len(pieces), high / len(pieces))
        return jnp.repeat(jnp.exp(heights), shape[axis_at] // blocks).reshape((-1,) + (1,) * (len(shape) - axis_at - 1))

    level = one(*pieces[0])
    for cut in pieces[1:]:
        level = level * one(*cut)
    return level


def profile(amount, total, most, lean):
    loads = [(1 << 20) // math.isqrt(rank ** lean) + 1 for rank in range(2, amount + 1)]
    rest, holding = total - most - (amount - 1), [1] * (amount - 1)
    while rest > 0:
        free = [i for i in range(amount - 1) if holding[i] < most]
        pool, remaining = sum([loads[i] for i in free]), rest
        for i in free:
            more = min(most - holding[i], max(1, remaining * loads[i] // pool), rest)
            holding[i] = holding[i] + more
            rest = rest - more
    return np.array([most] + holding)


def ragged_sizes(stream_key, count, total, most, lean):
    if count == 2:
        one = jax.random.randint(stream_key, (), max(1, total - most), min(most, total - 1) + 1)
        return jnp.stack([one, total - one])
    tallies = jnp.asarray(profile(count, total, most, lean), jnp.int32)
    couples = (count - 1) // 2
    donor, receiver = tallies[1:1 + 2 * couples:2], tallies[2:2 + 2 * couples:2]
    margin = jnp.minimum(donor - 1, most - receiver)
    shifted = jax.random.randint(jax.random.fold_in(stream_key, 1), (couples,), 0, 1 << 20) % (margin + 1)
    tallies = tallies.at[1:1 + 2 * couples:2].set(donor - shifted).at[2:2 + 2 * couples:2].set(receiver + shifted)
    return tallies[jax.random.permutation(jax.random.fold_in(stream_key, 2), count)]


def noise(rng, dims, spread, most, pieces=(), kind=jnp.bfloat16):
    values = spread * jax.random.normal(rng, dims, jnp.float32)
    if pieces:
        values = values * steps_of(rng, dims, pieces, -0.22, 0.18)
    return jnp.clip(values, -most, most).astype(kind)


def setup_inputs(seed: int = 0) -> dict:
    key_list = jax.random.split(jax.random.key(seed), 7)
    return {
        "queries": draw_queries(jax.random.fold_in(key_list[6], 71), 0),
        "keys": draw_keys(jax.random.fold_in(key_list[6], 71), 0),
        "values": noise(key_list[2], (TOKENS, KVH * HD), 1.0, 6.0, ((0, 32),)),
        "doc_lengths": ragged_sizes(key_list[3], DOCS, TOKENS, MAXDOC, 2).astype(jnp.int32),
        "fq_weight": draw_fq_weight(jax.random.fold_in(key_list[6], 71), 0),
        "fk_weight": draw_fk_weight(jax.random.fold_in(key_list[6], 71), 0),
    }


NEG = -1e30


def doc_index(positions, starts):
    return jnp.sum((starts[None, :] <= positions[:, None]).astype(jnp.int32), axis=1) - 1


def feature(inputs, weight):
    proj = jnp.dot(inputs, weight, preferred_element_type=jnp.float32)
    return jnp.concatenate([jax.nn.softmax(proj, axis=-1), jax.nn.softmax(-proj, axis=-1)], axis=-1).astype(jnp.bfloat16)


def head_pass(head, queries, keys, values, starts, fq_weight, fk_weight):
    group = QH // KVH
    q_head = lax.dynamic_slice_in_dim(queries, head * HD, HD, 1)
    k_head = lax.dynamic_slice_in_dim(keys, (head // group) * HD, HD, 1)
    v_head = lax.dynamic_slice_in_dim(values, (head // group) * HD, HD, 1)
    blk = math.gcd(TOKENS, 512)
    span = min(MAXDOC + blk, TOKENS)
    blocks = TOKENS // blk
    scale = HD ** -0.5

    def teacher_block(index):
        q_start = index * blk
        k_start = jnp.clip(q_start + blk - span, 0, TOKENS - span).astype(jnp.int32)
        q_pos = q_start + jnp.arange(blk, dtype=jnp.int32)
        k_pos = k_start + jnp.arange(span, dtype=jnp.int32)
        q_rows = lax.dynamic_slice_in_dim(q_head, q_start, blk, 0)
        k_rows = lax.dynamic_slice_in_dim(k_head, k_start, span, 0)
        v_rows = lax.dynamic_slice_in_dim(v_head, k_start, span, 0)
        mask = (doc_index(q_pos, starts)[:, None] == doc_index(k_pos, starts)[None, :]) & (k_pos[None, :] <= q_pos[:, None])
        scores = jnp.dot(q_rows, k_rows.T, preferred_element_type=jnp.float32) * scale
        scores = jnp.where(mask, scores, NEG)
        peak = jnp.max(scores, axis=1)
        weights = jnp.where(mask, jnp.exp(scores - peak[:, None]), 0.0)
        total = jnp.sum(weights, axis=1)
        return jnp.dot(weights.astype(jnp.bfloat16), v_rows, preferred_element_type=jnp.float32) / total[:, None]

    teacher = lax.map(teacher_block, jnp.arange(blocks, dtype=jnp.int32)).reshape(TOKENS, HD)
    query_feature_map = feature(q_head, fq_weight[head])
    key_feature_map = feature(k_head, fk_weight[head])

    def student_block(carry, index):
        state, norm_state = carry
        q_start = index * blk
        positions = q_start + jnp.arange(blk, dtype=jnp.int32)
        docs = doc_index(positions, starts)
        fq = lax.dynamic_slice_in_dim(query_feature_map, q_start, blk, 0)
        fk = lax.dynamic_slice_in_dim(key_feature_map, q_start, blk, 0)
        v_rows = lax.dynamic_slice_in_dim(v_head, q_start, blk, 0)
        mask = (docs[:, None] == docs[None, :]) & (positions[None, :] <= positions[:, None])
        score_matrix = jnp.where(mask, jnp.dot(fq, fk.T, preferred_element_type=jnp.float32), 0.0)
        numer = jnp.dot(score_matrix, v_rows.astype(jnp.float32), precision=lax.Precision.HIGHEST)
        denom = jnp.sum(score_matrix, axis=1)
        prev_doc = doc_index(jnp.reshape(q_start - 1, (1,)).astype(jnp.int32), starts)[0]
        carried = (docs == prev_doc).astype(jnp.float32)
        fq_wide = fq.astype(jnp.float32)
        numer = numer + carried[:, None] * jnp.dot(fq_wide, state, precision=lax.Precision.HIGHEST)
        denom = denom + carried * jnp.dot(fq_wide, norm_state, precision=lax.Precision.HIGHEST)
        last_mask = (docs == docs[-1]).astype(jnp.bfloat16)
        fk_last = fk * last_mask[:, None]
        inside = jnp.sum(((starts >= q_start) & (starts < q_start + blk)).astype(jnp.int32))
        keep = (inside == 0).astype(jnp.float32)
        state = keep * state + jnp.dot(fk_last.T, v_rows, preferred_element_type=jnp.float32)
        norm_state = keep * norm_state + jnp.sum(fk_last.astype(jnp.float32), axis=0)
        return (state, norm_state), numer / denom[:, None]

    init = (jnp.zeros((2 * FH, HD), jnp.float32), jnp.zeros((2 * FH,), jnp.float32))
    ignored, student = lax.scan(student_block, init, jnp.arange(blocks, dtype=jnp.int32))
    return teacher - student.reshape(TOKENS, HD)


def reference(queries, keys, values, doc_lengths, fq_weight, fk_weight):
    starts = (jnp.cumsum(doc_lengths) - doc_lengths).astype(jnp.int32)
    residuals = lax.map(lambda head: head_pass(head, queries, keys, values, starts, fq_weight, fk_weight), jnp.arange(QH, dtype=jnp.int32))
    residual = jnp.transpose(residuals, (1, 0, 2)).reshape(TOKENS, QH * HD)
    token_loss = jnp.sum(jnp.mean(residuals * residuals, axis=2), axis=0)
    return residual, token_loss
```

```python
import math

import jax
import jax.numpy as jnp
from jax import lax
from jax.experimental import pallas as pl
from jax.experimental.pallas import tpu as pltpu
from jax.sharding import Mesh
from jax.sharding import PartitionSpec as P

QH = 64
KVH = 8
MAXDOC = 2048
CHIP = ("seq_0", "seq_1")
CORE = "seq_2"
SEQ = (*CHIP, CORE)
NEG = -1e30
LOG2E = math.log2(math.e)
NT = (((1,), (1,)), ((), ()))


def dot(a, b, dims=(((1,), (0,)), ((), ()))):
    return lax.dot_general(a, b, dims, preferred_element_type=jnp.float32)


def split_dot(a, b):
    high = a.astype(jnp.bfloat16)
    low = (a - high.astype(jnp.float32)).astype(jnp.bfloat16)
    return dot(high, b) + dot(low, b)


def doc_start(doc_ref, pos):
    start = jnp.zeros_like(pos)
    at = jnp.int32(0)
    for d in range(doc_ref.shape[0]):
        start = jnp.where(pos >= at, at, start)
        at = at + doc_ref[d]
    return start


def softmaxes(proj, axis):
    p = proj * LOG2E
    up = jnp.exp2(p - jnp.max(p, axis=axis, keepdims=True))
    down = jnp.exp2(jnp.min(p, axis=axis, keepdims=True) - p)
    up = up * (1.0 / jnp.sum(up, axis=axis, keepdims=True))
    down = down * (1.0 / jnp.sum(down, axis=axis, keepdims=True))
    return jnp.concatenate([up.astype(jnp.bfloat16), down.astype(jnp.bfloat16)], axis=axis)


def with_ones(v):
    return jnp.concatenate([v, jnp.ones_like(v)], axis=1)


def own_kernel(at_ref, doc_ref, q_ref, k_ref, v_ref, fq_ref, fk_ref, lhs_ref, sd_ref, phi_ref, nd_ref):
    heads, hd, _ = fq_ref.shape
    rows = q_ref.shape[0]
    anchor = (2 * at_ref[0] + at_ref[1]) * rows
    q_pos = anchor + lax.broadcasted_iota(jnp.int32, (rows, 1), 0)
    k_pos = anchor + lax.broadcasted_iota(jnp.int32, (1, rows), 1)
    mask = (k_pos >= doc_start(doc_ref, q_pos)) & (k_pos <= q_pos)
    k = k_ref[...]
    v = with_ones(v_ref[...])
    for h in range(heads):
        q = q_ref[:, h * hd:(h + 1) * hd]
        lhs_ref[h * rows:(h + 1) * rows, :] = q
        fk_t = jnp.transpose(fk_ref[h].astype(jnp.float32)).astype(jnp.bfloat16)
        lhs_ref[heads * rows + h * hd:heads * rows + (h + 1) * hd, :] = fk_t
        sd_ref[h] = jnp.where(mask, dot(q, k, NT) * (hd ** -0.5 * LOG2E), NEG)
        phi_q = softmaxes(dot(q, fq_ref[h]), 1)
        phi_ref[h] = phi_q
        phi_k = softmaxes(dot(fk_t, k, NT), 0)
        affinity = jnp.where(mask, dot(phi_q, phi_k), 0.0)
        nd_ref[h] = split_dot(affinity, v)


def earlier_kernel(
    at_ref, doc_ref, a_ref, b_ref, lhs_ref, sd_ref, phi_ref, nd_ref, res_ref, loss_ref,
    s_scr, state_scr, max_scr, acc_scr,
):
    heads, rows, hd = sd_ref.shape
    chip, core = at_ref[0], at_ref[1]
    anchor = (2 * chip + core) * rows
    first = doc_start(doc_ref, anchor)
    c0 = first // (2 * rows)
    c1 = jnp.where(first < anchor, (anchor - 1) // (2 * rows) + 1, c0)
    qr = heads * rows
    scale = hd ** -0.5 * LOG2E
    state_scr[...] = jnp.zeros_like(state_scr)
    acc_scr[...] = jnp.zeros_like(acc_scr)
    max_scr[...] = jnp.full_like(max_scr, NEG)

    def positions(c, shape, dim):
        lane = lax.broadcasted_iota(jnp.int32, shape, dim)
        own = (2 * c + core) * rows + lane
        other = (2 * c + 1 - core) * rows + lane - rows
        pos = jnp.where(lane < rows, own, other)
        return (pos >= first) & (pos < anchor)

    def both(c, at):
        return jnp.concatenate([a_ref[c, :, at:at + hd], b_ref[c, :, at:at + hd]], axis=0)

    def scan_keys(c, _):
        z = dot(lhs_ref[...], both(c, 0), NT)
        s = jnp.where(positions(c, (1, 2 * rows), 1), z[:qr] * scale, NEG)
        s_scr[c - c0] = s
        max_scr[...] = jnp.maximum(max_scr[...], jnp.maximum(s[:, :rows], s[:, rows:]))
        seen = jnp.where(positions(c, (2 * rows, 1), 0), 1.0, 0.0).astype(jnp.bfloat16)
        v = with_ones(both(c, hd)) * seen
        for h in range(heads):
            phi_k = softmaxes(z[qr + h * hd:qr + (h + 1) * hd], 0)
            state_scr[h] += dot(phi_k, v)
        return _

    lax.fori_loop(c0, c1, scan_keys, 0)

    q_pos = anchor + lax.broadcasted_iota(jnp.int32, (rows, 1), 0)
    carried = jnp.broadcast_to(jnp.where(doc_start(doc_ref, q_pos) == first, 1.0, 0.0), (rows, hd)) > 0.5
    v_own = with_ones(a_ref[chip, :, hd:2 * hd])
    for h in range(heads):
        at = slice(h * rows, (h + 1) * rows)
        sd = sd_ref[h]
        off = jnp.broadcast_to(jnp.max(max_scr[at], axis=1, keepdims=True), (rows, hd))
        peak = jnp.maximum(
            jnp.broadcast_to(jnp.max(sd, axis=1, keepdims=True), (rows, hd)), jnp.where(carried, off, NEG)
        )
        acc_scr[at] = dot(jnp.exp2(sd - peak).astype(jnp.bfloat16), v_own)
        max_scr[at] = jnp.where(carried, peak, -NEG)

    def weigh(c, _):
        peak = max_scr[...]
        s = s_scr[c - c0]
        w = jnp.concatenate(
            [jnp.exp2(s[:, :rows] - peak).astype(jnp.bfloat16), jnp.exp2(s[:, rows:] - peak).astype(jnp.bfloat16)],
            axis=1,
        )
        acc_scr[...] += dot(w, with_ones(both(c, hd)))
        return _

    lax.fori_loop(c0, c1, weigh, 0)

    squares = jnp.zeros((rows, hd), jnp.float32)
    for h in range(heads):
        acc = acc_scr[h * rows:(h + 1) * rows]
        state = state_scr[h]
        high = state.astype(jnp.bfloat16)
        low = (state - high.astype(jnp.float32)).astype(jnp.bfloat16)
        phi = phi_ref[h]
        nd = dot(phi, high) + dot(phi, low)
        own = nd_ref[h]
        numer = own[:, :hd] + jnp.where(carried, nd[:, :hd], 0.0)
        denom = own[:, hd:] + jnp.where(carried, nd[:, hd:], 0.0)
        residual = acc[:, :hd] / acc[:, hd:] - numer / denom
        res_ref[:, h * hd:(h + 1) * hd] = residual
        squares = squares + residual * residual
    loss = jnp.sum(jnp.transpose(squares), axis=0, keepdims=True) * (1.0 / hd)
    loss_ref[...] = jnp.broadcast_to(loss, loss_ref.shape)


def body(queries, keys, values, doc_lengths, fq_weight, fk_weight):
    rows = queries.shape[0]
    heads, hd, _ = fq_weight.shape
    kv_head = lax.axis_index("head") * heads // (QH // KVH)
    chip, core = lax.axis_index(CHIP), lax.axis_index(CORE)
    chips, planes = lax.axis_size(CHIP), lax.axis_size("head")
    at = jnp.stack([chip, core]).astype(jnp.int32)
    k_own = lax.dynamic_slice_in_dim(keys, kv_head * hd, hd, 1)
    v_own = lax.dynamic_slice_in_dim(values, kv_head * hd, hd, 1)
    kv = jnp.concatenate([k_own, v_own], axis=1)
    a = lax.all_to_all(jnp.broadcast_to(kv, (chips, *kv.shape)), CHIP, 0, 0, tiled=True)
    b = lax.ppermute(a, CORE, [(0, 1), (1, 0)])
    smem = pl.BlockSpec(memory_space=pltpu.SMEM)
    vmem = pl.BlockSpec(memory_space=pltpu.VMEM)
    params = pltpu.CompilerParams(vmem_limit_bytes=32 * 1024 * 1024)
    f32, bf16 = jnp.float32, jnp.bfloat16
    lhs, sd, phi, nd = pl.pallas_call(
        own_kernel,
        out_shape=(
            jax.ShapeDtypeStruct((heads * (rows + hd), hd), bf16),
            jax.ShapeDtypeStruct((heads, rows, rows), f32),
            jax.ShapeDtypeStruct((heads, rows, 2 * hd), bf16),
            jax.ShapeDtypeStruct((heads, rows, 2 * hd), f32),
        ),
        in_specs=[smem, smem] + [vmem] * 5,
        out_specs=(vmem,) * 4,
        compiler_params=params,
        cost_estimate=pl.CostEstimate(flops=10**9, bytes_accessed=2 * 10**6, transcendentals=10**6),
        name="own_block",
    )(at, doc_lengths, queries, k_own, v_own, fq_weight, fk_weight)
    steps = MAXDOC // (2 * rows) + 1
    residual, loss = pl.pallas_call(
        earlier_kernel,
        out_shape=(
            jax.ShapeDtypeStruct((rows, heads * hd), f32),
            jax.ShapeDtypeStruct((planes, rows), f32),
        ),
        in_specs=[smem, smem] + [vmem] * 6,
        out_specs=(vmem, vmem),
        scratch_shapes=[
            pltpu.VMEM((steps, heads * rows, 2 * rows), f32),
            pltpu.VMEM((heads, 2 * hd, 2 * hd), f32),
            pltpu.VMEM((heads * rows, rows), f32),
            pltpu.VMEM((heads * rows, 2 * hd), f32),
        ],
        compiler_params=params,
        cost_estimate=pl.CostEstimate(flops=4 * 10**9, bytes_accessed=4 * 10**6, transcendentals=4 * 10**6),
        name="earlier_blocks",
    )(at, doc_lengths, a, b, lhs, sd, phi, nd)
    parts = lax.all_to_all(loss, "head", 0, 0, tiled=True)
    return residual, jnp.sum(parts, axis=0)


def solution(mesh):
    split = Mesh(mesh.devices.reshape(4, 4, 2, mesh.shape["head"]), (*SEQ, "head"))
    placed = (
        P(SEQ, "head"),
        P(SEQ, None),
        P(SEQ, None),
        P(),
        P("head", None, None),
        P("head", None, None),
    )
    return jax.shard_map(
        body, mesh=split, in_specs=placed, out_specs=(P(SEQ, "head"), P(SEQ)), check_vma=False
    )
```

```python
import math

import jax
import jax.numpy as jnp
from jax import lax
from jax.experimental import pallas as pl
from jax.experimental.pallas import tpu as pltpu
from jax.sharding import Mesh
from jax.sharding import PartitionSpec as P

QH = 64
KVH = 8
MAXDOC = 2048
CHIP = ("seq_0", "seq_1")
CORE = "seq_2"
SEQ = (*CHIP, CORE)
NEG = -1e30
LOG2E = math.log2(math.e)
NT = (((1,), (1,)), ((), ()))


def dot(a, b, dims=(((1,), (0,)), ((), ()))):
    return lax.dot_general(a, b, dims, preferred_element_type=jnp.float32)


def split_dot(a, b):
    high = a.astype(jnp.bfloat16)
    low = (a - high.astype(jnp.float32)).astype(jnp.bfloat16)
    return dot(high, b) + dot(low, b)


def doc_start(doc_ref, pos):
    start = jnp.zeros_like(pos)
    at = jnp.int32(0)
    for d in range(doc_ref.shape[0]):
        start = jnp.where(pos >= at, at, start)
        at = at + doc_ref[d]
    return start


def softmaxes(proj, axis):
    p = proj * LOG2E
    up = jnp.exp2(p - jnp.max(p, axis=axis, keepdims=True))
    down = jnp.exp2(jnp.min(p, axis=axis, keepdims=True) - p)
    up = up * (1.0 / jnp.sum(up, axis=axis, keepdims=True))
    down = down * (1.0 / jnp.sum(down, axis=axis, keepdims=True))
    return jnp.concatenate([up.astype(jnp.bfloat16), down.astype(jnp.bfloat16)], axis=axis)


def with_ones(v):
    return jnp.concatenate([v, jnp.ones_like(v)], axis=1)


def send_kernel(k_ref, v_ref, send_ref):
    hd = k_ref.shape[1]
    k_t = jnp.transpose(k_ref[...].astype(jnp.float32)).astype(jnp.bfloat16)
    for c in range(send_ref.shape[0]):
        send_ref[c, :, :hd] = k_t
        send_ref[c, :, hd:] = v_ref[...]


def own_kernel(at_ref, doc_ref, q_ref, k_ref, v_ref, fq_ref, fk_ref, lhs_ref, sd_ref, phi_ref, nd_ref, v_own_ref):
    heads, hd, _ = fq_ref.shape
    rows = q_ref.shape[0]
    anchor = (2 * at_ref[0] + at_ref[1]) * rows
    q_pos = anchor + lax.broadcasted_iota(jnp.int32, (rows, 1), 0)
    k_pos = anchor + lax.broadcasted_iota(jnp.int32, (1, rows), 1)
    mask = (k_pos >= doc_start(doc_ref, q_pos)) & (k_pos <= q_pos)
    k = k_ref[...]
    v = with_ones(v_ref[...])
    v_own_ref[...] = v
    for h in range(heads):
        q = q_ref[:, h * hd:(h + 1) * hd]
        lhs_ref[h * rows:(h + 1) * rows, :] = q
        fk_t = jnp.transpose(fk_ref[h].astype(jnp.float32)).astype(jnp.bfloat16)
        lhs_ref[heads * rows + h * hd:heads * rows + (h + 1) * hd, :] = fk_t
        sd_ref[h] = jnp.where(mask, dot(q, k, NT) * (hd ** -0.5 * LOG2E), NEG)
        phi_q = softmaxes(dot(q, fq_ref[h]), 1)
        phi_ref[h] = phi_q
        phi_k = softmaxes(dot(fk_t, k, NT), 0)
        affinity = jnp.where(mask, dot(phi_q, phi_k), 0.0)
        nd_ref[h] = split_dot(affinity, v)


def scan_keys(kv_ref, lhs_ref, s_ref, max_ref, state_ref, c0, parity, first, anchor, before):
    heads, rows, hd = state_ref.shape[0], max_ref.shape[1], kv_ref.shape[1]
    qr = heads * rows
    scale = hd ** -0.5 * LOG2E

    def visible(c, shape, dim):
        lane = lax.broadcasted_iota(jnp.int32, shape, dim)
        pos = (2 * c + parity) * rows + lane + jnp.where(lane < rows, 0, rows)
        return (pos >= first) & (pos < anchor)

    for i in range(s_ref.shape[0]):
        c = c0 + 2 * i
        low, high = jnp.maximum(c, 0), jnp.maximum(c + 1, 0)
        k_t = jnp.concatenate([kv_ref[low, :, :hd], kv_ref[high, :, :hd]], axis=1)
        v = jnp.concatenate([kv_ref[low, :, hd:], kv_ref[high, :, hd:]], axis=0)
        z = dot(lhs_ref[...], k_t)
        s = jnp.where(visible(c, (1, 2 * rows), 1), z[:qr] * scale, NEG)
        s_ref[i] = s
        m = jnp.maximum(s[:, :rows], s[:, rows:])
        if i > 0:
            m = jnp.maximum(max_ref[...], m)
        elif before is not None:
            m = jnp.maximum(before[0][...], m)
        max_ref[...] = m
        v = with_ones(v) * jnp.where(visible(c, (2 * rows, 1), 0), 1.0, 0.0).astype(jnp.bfloat16)
        for h in range(heads):
            d = dot(softmaxes(z[qr + h * hd:qr + (h + 1) * hd], 0), v)
            if i > 0:
                d = state_ref[h] + d
            elif before is not None:
                d = before[1][h] + d
            state_ref[h] = d


def same_core_kernel(at_ref, doc_ref, a_ref, lhs_ref, s_ref, max_ref, state_ref):
    rows = max_ref.shape[1]
    chip, core = at_ref[0], at_ref[1]
    anchor = (2 * chip + core) * rows
    first = doc_start(doc_ref, anchor)
    scan_keys(a_ref, lhs_ref, s_ref, max_ref, state_ref, chip - 2 * s_ref.shape[0], core, first, anchor, None)


def other_core_kernel(
    at_ref, doc_ref, a_ref, b_ref, lhs_ref, sa_ref, max_a_ref, state_a_ref, sd_ref, phi_ref, nd_ref, v_own_ref,
    res_ref, loss_ref, sb_ref, max_ref, state_ref, acc_ref,
):
    heads, rows, hd = sd_ref.shape
    chip, core = at_ref[0], at_ref[1]
    anchor = (2 * chip + core) * rows
    first = doc_start(doc_ref, anchor)
    steps = sb_ref.shape[0]
    a0, b0 = chip - 2 * steps, chip - 2 * steps + core
    scan_keys(b_ref, lhs_ref, sb_ref, max_ref, state_ref, b0, 1 - core, first, anchor, (max_a_ref, state_a_ref))

    q_pos = anchor + lax.broadcasted_iota(jnp.int32, (rows, 1), 0)
    carried = jnp.broadcast_to(jnp.where(doc_start(doc_ref, q_pos) == first, 1.0, 0.0), (rows, hd)) > 0.5
    for h in range(heads):
        at = slice(h * rows, (h + 1) * rows)
        sd = sd_ref[h]
        off = jnp.broadcast_to(jnp.max(max_ref[at], axis=1, keepdims=True), (rows, hd))
        peak = jnp.maximum(
            jnp.broadcast_to(jnp.max(sd, axis=1, keepdims=True), (rows, hd)), jnp.where(carried, off, NEG)
        )
        acc_ref[at] = dot(jnp.exp2(sd - peak).astype(jnp.bfloat16), v_own_ref[...])
        max_ref[at] = jnp.where(carried, peak, -NEG)

    weights, seen = [], []
    for kv_ref, s_ref, c0 in ((a_ref, sa_ref, a0), (b_ref, sb_ref, b0)):
        for i in range(steps):
            c = c0 + 2 * i
            low, high = jnp.maximum(c, 0), jnp.maximum(c + 1, 0)
            peak = max_ref[...]
            s = s_ref[i]
            weights.append(jnp.exp2(s[:, :rows] - peak).astype(jnp.bfloat16))
            weights.append(jnp.exp2(s[:, rows:] - peak).astype(jnp.bfloat16))
            seen.append(with_ones(kv_ref[low, :, hd:]))
            seen.append(with_ones(kv_ref[high, :, hd:]))
    acc_ref[...] += dot(jnp.concatenate(weights, axis=1), jnp.concatenate(seen, axis=0))

    squares = jnp.zeros((rows, hd), jnp.float32)
    for h in range(heads):
        acc = acc_ref[h * rows:(h + 1) * rows]
        state = state_ref[h]
        high = state.astype(jnp.bfloat16)
        low = (state - high.astype(jnp.float32)).astype(jnp.bfloat16)
        phi = phi_ref[h]
        nd = dot(phi, high) + dot(phi, low)
        own = nd_ref[h]
        numer = own[:, :hd] + jnp.where(carried, nd[:, :hd], 0.0)
        denom = own[:, hd:] + jnp.where(carried, nd[:, hd:], 0.0)
        residual = acc[:, :hd] / acc[:, hd:] - numer / denom
        res_ref[:, h * hd:(h + 1) * hd] = residual
        squares = squares + residual * residual
    loss = jnp.sum(jnp.transpose(squares), axis=0, keepdims=True) * (1.0 / hd)
    loss_ref[...] = jnp.broadcast_to(loss, loss_ref.shape)


F32, BF16 = jnp.float32, jnp.bfloat16
SMEM = pl.BlockSpec(memory_space=pltpu.SMEM)
VMEM = pl.BlockSpec(memory_space=pltpu.VMEM)


def shapes(*items):
    return tuple(jax.ShapeDtypeStruct(s, t) for s, t in items)


def params(mib):
    return pltpu.CompilerParams(vmem_limit_bytes=mib * 1024 * 1024)


def to_send(k_own, v_own, chips):
    rows, hd = k_own.shape
    return pl.pallas_call(
        send_kernel,
        out_shape=jax.ShapeDtypeStruct((chips, hd, rows + hd), BF16),
        in_specs=[VMEM, VMEM],
        out_specs=VMEM,
        compiler_params=params(8),
        name="to_send",
    )(k_own, v_own)


def own_block(at, doc_lengths, queries, k_own, v_own, fq_weight, fk_weight):
    rows = queries.shape[0]
    heads, hd, _ = fq_weight.shape
    return pl.pallas_call(
        own_kernel,
        out_shape=shapes(
            ((heads * (rows + hd), hd), BF16),
            ((heads, rows, rows), F32),
            ((heads, rows, 2 * hd), BF16),
            ((heads, rows, 2 * hd), F32),
            ((rows, 2 * hd), BF16),
        ),
        in_specs=[SMEM, SMEM] + [VMEM] * 5,
        out_specs=(VMEM,) * 5,
        compiler_params=params(16),
        cost_estimate=pl.CostEstimate(flops=10**9, bytes_accessed=2 * 10**6, transcendentals=10**6),
        name="own_block",
    )(at, doc_lengths, queries, k_own, v_own, fq_weight, fk_weight)


def same_core(at, doc_lengths, a, lhs, heads):
    rows = hd = lhs.shape[1]
    steps = MAXDOC // (4 * rows)
    return pl.pallas_call(
        same_core_kernel,
        out_shape=shapes(
            ((steps, heads * rows, 2 * rows), F32), ((heads * rows, rows), F32), ((heads, 2 * hd, 2 * hd), F32)
        ),
        in_specs=[SMEM, SMEM, VMEM, VMEM],
        out_specs=(VMEM,) * 3,
        compiler_params=params(16),
        cost_estimate=pl.CostEstimate(flops=2 * 10**9, bytes_accessed=4 * 10**6, transcendentals=2 * 10**6),
        name="same_core",
    )(at, doc_lengths, a, lhs)


def other_core(at, doc_lengths, a, b, lhs, sa, max_a, state_a, sd, phi, nd, v_own, planes):
    heads, rows, hd = sd.shape
    return pl.pallas_call(
        other_core_kernel,
        out_shape=shapes(((rows, heads * hd), F32), ((planes, rows), F32)),
        in_specs=[SMEM, SMEM] + [VMEM] * 10,
        out_specs=(VMEM, VMEM),
        scratch_shapes=[
            pltpu.VMEM(sa.shape, F32),
            pltpu.VMEM(max_a.shape, F32),
            pltpu.VMEM(state_a.shape, F32),
            pltpu.VMEM((heads * rows, 2 * hd), F32),
        ],
        compiler_params=params(24),
        cost_estimate=pl.CostEstimate(flops=4 * 10**9, bytes_accessed=4 * 10**6, transcendentals=4 * 10**6),
        name="other_core",
    )(at, doc_lengths, a, b, lhs, sa, max_a, state_a, sd, phi, nd, v_own)


def body(queries, keys, values, doc_lengths, fq_weight, fk_weight):
    heads, hd, _ = fq_weight.shape
    kv_head = lax.axis_index("head") * heads // (QH // KVH)
    at = jnp.stack([lax.axis_index(CHIP), lax.axis_index(CORE)]).astype(jnp.int32)
    k_own = lax.dynamic_slice_in_dim(keys, kv_head * hd, hd, 1)
    v_own = lax.dynamic_slice_in_dim(values, kv_head * hd, hd, 1)
    send = to_send(k_own, v_own, lax.axis_size(CHIP))
    a = lax.all_to_all(send, CHIP, 0, 0, tiled=True)
    lhs, sd, phi, nd, v_own = own_block(at, doc_lengths, queries, k_own, v_own, fq_weight, fk_weight)
    a, lhs = lax.optimization_barrier((a, lhs))
    b = lax.ppermute(a, CORE, [(0, 1), (1, 0)])
    sa, max_a, state_a = same_core(at, doc_lengths, a, lhs, heads)
    residual, loss = other_core(
        at, doc_lengths, a, b, lhs, sa, max_a, state_a, sd, phi, nd, v_own, lax.axis_size("head")
    )
    parts = lax.all_to_all(loss, "head", 0, 0, tiled=True)
    return residual, jnp.sum(parts, axis=0)


def solution(mesh):
    split = Mesh(mesh.devices.reshape(4, 4, 2, mesh.shape["head"]), (*SEQ, "head"))
    placed = (
        P(SEQ, "head"),
        P(SEQ, None),
        P(SEQ, None),
        P(),
        P("head", None, None),
        P("head", None, None),
    )
    return jax.shard_map(
        body, mesh=split, in_specs=placed, out_specs=(P(SEQ, "head"), P(SEQ)), check_vma=False
    )
```

```python
import math

import jax
import jax.numpy as jnp
from jax import lax
from jax.experimental import pallas as pl
from jax.experimental.pallas import tpu as pltpu
from jax.sharding import Mesh
from jax.sharding import PartitionSpec as P

MAXDOC = 2048
CHIP = ("seq_0", "seq_1")
CORE = "seq_2"
SEQ = (*CHIP, CORE)
NEG = -1e30
FIRST_CHIP, FIRST_PLANE = 10, 8
LOG2E = math.log2(math.e)


def dot(a, b):
    return jnp.dot(a, b, preferred_element_type=jnp.float32)


def split_dot(a, b):
    high = a.astype(jnp.bfloat16)
    low = (a - high.astype(jnp.float32)).astype(jnp.bfloat16)
    return dot(high, b) + dot(low, b)


def slot(c, chips):
    return lax.rem(jnp.maximum(c, 0) + (chips - FIRST_CHIP), chips)


def doc_start(doc_ref, pos):
    start = jnp.zeros_like(pos)
    at = jnp.int32(0)
    for d in range(doc_ref.shape[0]):
        start = jnp.where(pos >= at, at, start)
        at = at + doc_ref[d]
    return start


def softmaxes(proj, axis):
    p = proj * LOG2E
    up = jnp.exp2(p - jnp.max(p, axis=axis, keepdims=True))
    down = jnp.exp2(jnp.min(p, axis=axis, keepdims=True) - p)
    up = up * (1.0 / jnp.sum(up, axis=axis, keepdims=True))
    down = down * (1.0 / jnp.sum(down, axis=axis, keepdims=True))
    return jnp.concatenate([up.astype(jnp.bfloat16), down.astype(jnp.bfloat16)], axis=axis)


def with_ones(v):
    return jnp.concatenate([v, jnp.ones_like(v)], axis=1)


def send_kernel(keys_ref, values_ref, send_ref, own_ref, k_ref, in_sem, out_sem):
    chips, hd, _ = send_ref.shape
    rows = k_ref.shape[0]
    column = lax.axis_index("head") * keys_ref.shape[1] // (hd * lax.axis_size("head"))
    at = pl.ds(pl.multiple_of(column * hd, hd), hd)
    get_k = pltpu.make_async_copy(keys_ref.at[:, at], k_ref, in_sem.at[0])
    get_v = pltpu.make_async_copy(values_ref.at[:, at], own_ref.at[:, pl.ds(rows, hd)], in_sem.at[1])
    get_k.start()
    get_v.start()
    get_k.wait()
    own_ref[:, :rows] = jnp.transpose(k_ref[...].astype(jnp.float32)).astype(jnp.bfloat16)
    get_v.wait()
    puts = [pltpu.make_async_copy(own_ref, send_ref.at[c], out_sem.at[c]) for c in range(chips)]
    for put in puts:
        put.start()
    for put in puts:
        put.wait()


def own_kernel(at_ref, doc_ref, q_ref, kv_ref, fq_ref, fk_ref, lhs_ref, sd_ref, peak_ref, phi_ref, nd_ref, v_own_ref):
    heads, hd, _ = fq_ref.shape
    rows = q_ref.shape[0]
    anchor = (2 * at_ref[0] + at_ref[1]) * rows
    q_pos = anchor + lax.broadcasted_iota(jnp.int32, (rows, 1), 0)
    k_pos = anchor + lax.broadcasted_iota(jnp.int32, (1, rows), 1)
    mask = (k_pos >= doc_start(doc_ref, q_pos)) & (k_pos <= q_pos)
    k_t = kv_ref[:, :rows]
    v = with_ones(kv_ref[:, rows:])
    v_own_ref[...] = v
    for h in range(heads):
        q = q_ref[:, h * hd:(h + 1) * hd]
        lhs_ref[h * rows:(h + 1) * rows, :] = q
        fk_t = jnp.transpose(fk_ref[h].astype(jnp.float32)).astype(jnp.bfloat16)
        lhs_ref[heads * rows + h * hd:heads * rows + (h + 1) * hd, :] = fk_t
        sd = jnp.where(mask, dot(q, k_t) * (hd ** -0.5 * LOG2E), NEG)
        sd_ref[h] = sd
        peak_ref[h] = jnp.broadcast_to(jnp.max(sd, axis=1, keepdims=True), sd.shape)
        phi_q = softmaxes(dot(q, fq_ref[h]), 1)
        phi_ref[h] = phi_q
        phi_k = softmaxes(dot(fk_t, k_t), 0)
        affinity = jnp.where(mask, dot(phi_q, phi_k), 0.0)
        nd_ref[h] = split_dot(affinity, v)


def scan_keys(kv_ref, lhs_ref, s_ref, max_ref, state_ref, c0, parity, first, anchor, before):
    heads, rows, hd = state_ref.shape[0], max_ref.shape[1], kv_ref.shape[1]
    qr = heads * rows
    scale = hd ** -0.5 * LOG2E

    def visible(c, shape, dim):
        lane = lax.broadcasted_iota(jnp.int32, shape, dim)
        pos = (2 * c + parity) * rows + lane + jnp.where(lane < rows, 0, rows)
        return (pos >= first) & (pos < anchor)

    for i in range(s_ref.shape[0]):
        c = c0 + 2 * i
        low, high = slot(c, kv_ref.shape[0]), slot(c + 1, kv_ref.shape[0])
        k_t = jnp.concatenate([kv_ref[low, :, :hd], kv_ref[high, :, :hd]], axis=1)
        v = jnp.concatenate([kv_ref[low, :, hd:], kv_ref[high, :, hd:]], axis=0)
        z = dot(lhs_ref[...], k_t)
        s = jnp.where(visible(c, (1, 2 * rows), 1), z[:qr] * scale, NEG)
        s_ref[i] = s
        m = jnp.maximum(s[:, :rows], s[:, rows:])
        if i > 0:
            m = jnp.maximum(max_ref[...], m)
        elif before is not None:
            m = jnp.maximum(before[0][...], m)
        max_ref[...] = m
        v = with_ones(v) * jnp.where(visible(c, (2 * rows, 1), 0), 1.0, 0.0).astype(jnp.bfloat16)
        for h in range(heads):
            d = dot(softmaxes(z[qr + h * hd:qr + (h + 1) * hd], 0), v)
            if i > 0:
                d = state_ref[h] + d
            elif before is not None:
                d = before[1][h] + d
            state_ref[h] = d


def same_core_kernel(at_ref, doc_ref, a_ref, lhs_ref, s_ref, max_ref, state_ref):
    rows = max_ref.shape[1]
    chip, core = at_ref[0], at_ref[1]
    anchor = (2 * chip + core) * rows
    first = doc_start(doc_ref, anchor)
    scan_keys(a_ref, lhs_ref, s_ref, max_ref, state_ref, chip - 2 * s_ref.shape[0], core, first, anchor, None)


def other_core_kernel(
    at_ref, doc_ref, a_ref, b_ref, lhs_ref, sa_ref, max_a_ref, state_a_ref, sd_ref, peak_ref, phi_ref, nd_ref, v_own_ref,
    res_ref, loss_ref, sb_ref, max_ref, state_ref, acc_ref,
):
    heads, rows, hd = sd_ref.shape
    chip, core = at_ref[0], at_ref[1]
    anchor = (2 * chip + core) * rows
    first = doc_start(doc_ref, anchor)
    steps = sb_ref.shape[0]
    a0, b0 = chip - 2 * steps, chip - 2 * steps + core
    scan_keys(b_ref, lhs_ref, sb_ref, max_ref, state_ref, b0, 1 - core, first, anchor, (max_a_ref, state_a_ref))

    q_pos = anchor + lax.broadcasted_iota(jnp.int32, (rows, 1), 0)
    carried = jnp.broadcast_to(jnp.where(doc_start(doc_ref, q_pos) == first, 1.0, 0.0), (rows, hd)) > 0.5
    for h in range(heads):
        at = slice(h * rows, (h + 1) * rows)
        sd = sd_ref[h]
        off = jnp.broadcast_to(jnp.max(max_ref[at], axis=1, keepdims=True), (rows, hd))
        peak = jnp.maximum(peak_ref[h], jnp.where(carried, off, NEG))
        acc_ref[at] = dot(jnp.exp2(sd - peak).astype(jnp.bfloat16), v_own_ref[...])
        max_ref[at] = jnp.where(carried, peak, -NEG)

    weights, seen = [], []
    for kv_ref, s_ref, c0 in ((a_ref, sa_ref, a0), (b_ref, sb_ref, b0)):
        for i in range(steps):
            c = c0 + 2 * i
            low, high = slot(c, kv_ref.shape[0]), slot(c + 1, kv_ref.shape[0])
            peak = max_ref[...]
            s = s_ref[i]
            weights.append(jnp.exp2(s[:, :rows] - peak).astype(jnp.bfloat16))
            weights.append(jnp.exp2(s[:, rows:] - peak).astype(jnp.bfloat16))
            seen.append(with_ones(kv_ref[low, :, hd:]))
            seen.append(with_ones(kv_ref[high, :, hd:]))
    acc_ref[...] += dot(jnp.concatenate(weights, axis=1), jnp.concatenate(seen, axis=0))

    squares = jnp.zeros((rows, hd), jnp.float32)
    for h in range(heads):
        acc = acc_ref[h * rows:(h + 1) * rows]
        state = state_ref[h]
        high = state.astype(jnp.bfloat16)
        low = (state - high.astype(jnp.float32)).astype(jnp.bfloat16)
        phi = phi_ref[h]
        nd = dot(phi, high) + dot(phi, low)
        own = nd_ref[h]
        numer = own[:, :hd] + jnp.where(carried, nd[:, :hd], 0.0)
        denom = own[:, hd:] + jnp.where(carried, nd[:, hd:], 0.0)
        residual = acc[:, :hd] / acc[:, hd:] - numer / denom
        res_ref[:, h * hd:(h + 1) * hd] = residual
        squares = squares + residual * residual
    loss = jnp.sum(jnp.transpose(squares), axis=0, keepdims=True) * (1.0 / hd)
    loss_ref[...] = jnp.broadcast_to(loss, loss_ref.shape)


F32, BF16 = jnp.float32, jnp.bfloat16
SMEM = pl.BlockSpec(memory_space=pltpu.SMEM)
VMEM = pl.BlockSpec(memory_space=pltpu.VMEM)
HBM = pl.BlockSpec(memory_space=pltpu.HBM)


def rotated(array, axis, first):
    size = lax.axis_size(axis)
    group = [(first + j) % size for j in range(size)]
    return lax.all_to_all(array, axis, 0, 0, tiled=True, axis_index_groups=[group])


def shapes(*items):
    return tuple(jax.ShapeDtypeStruct(s, t) for s, t in items)


def params(mib):
    return pltpu.CompilerParams(vmem_limit_bytes=mib * 1024 * 1024)


def to_send(keys, values, chips, hd):
    rows = keys.shape[0]
    return pl.pallas_call(
        send_kernel,
        out_shape=shapes(((chips, hd, rows + hd), BF16), ((hd, rows + hd), BF16)),
        in_specs=[HBM, HBM],
        out_specs=(HBM, VMEM),
        scratch_shapes=[
            pltpu.VMEM((rows, hd), BF16),
            pltpu.SemaphoreType.DMA((2,)),
            pltpu.SemaphoreType.DMA((chips,)),
        ],
        name="to_send",
    )(keys, values)


def own_block(at, doc_lengths, queries, kv_own, fq_weight, fk_weight):
    rows = queries.shape[0]
    heads, hd, _ = fq_weight.shape
    return pl.pallas_call(
        own_kernel,
        out_shape=shapes(
            ((heads * (rows + hd), hd), BF16),
            ((heads, rows, rows), F32),
            ((heads, rows, rows), F32),
            ((heads, rows, 2 * hd), BF16),
            ((heads, rows, 2 * hd), F32),
            ((rows, 2 * hd), BF16),
        ),
        in_specs=[SMEM, SMEM] + [VMEM] * 4,
        out_specs=(VMEM,) * 6,
        compiler_params=params(16),
        cost_estimate=pl.CostEstimate(flops=10**9, bytes_accessed=2 * 10**6, transcendentals=10**6),
        name="own_block",
    )(at, doc_lengths, queries, kv_own, fq_weight, fk_weight)


def same_core(at, doc_lengths, a, lhs, heads):
    rows = hd = lhs.shape[1]
    steps = MAXDOC // (4 * rows)
    return pl.pallas_call(
        same_core_kernel,
        out_shape=shapes(
            ((steps, heads * rows, 2 * rows), F32), ((heads * rows, rows), F32), ((heads, 2 * hd, 2 * hd), F32)
        ),
        in_specs=[SMEM, SMEM, VMEM, VMEM],
        out_specs=(VMEM,) * 3,
        compiler_params=params(16),
        cost_estimate=pl.CostEstimate(flops=2 * 10**9, bytes_accessed=4 * 10**6, transcendentals=2 * 10**6),
        name="same_core",
    )(at, doc_lengths, a, lhs)


def other_core(at, doc_lengths, a, b, lhs, sa, max_a, state_a, sd, peak, phi, nd, v_own, planes):
    heads, rows, hd = sd.shape
    return pl.pallas_call(
        other_core_kernel,
        out_shape=shapes(((rows, heads * hd), F32), ((planes, rows), F32)),
        in_specs=[SMEM, SMEM] + [VMEM] * 11,
        out_specs=(VMEM, VMEM),
        scratch_shapes=[
            pltpu.VMEM(sa.shape, F32),
            pltpu.VMEM(max_a.shape, F32),
            pltpu.VMEM(state_a.shape, F32),
            pltpu.VMEM((heads * rows, 2 * hd), F32),
        ],
        compiler_params=params(24),
        cost_estimate=pl.CostEstimate(flops=4 * 10**9, bytes_accessed=4 * 10**6, transcendentals=4 * 10**6),
        name="other_core",
    )(at, doc_lengths, a, b, lhs, sa, max_a, state_a, sd, peak, phi, nd, v_own)


def body(queries, keys, values, doc_lengths, fq_weight, fk_weight):
    heads, hd, _ = fq_weight.shape
    at = jnp.stack([lax.axis_index(CHIP), lax.axis_index(CORE)]).astype(jnp.int32)
    send, kv_own = to_send(keys, values, lax.axis_size(CHIP), hd)
    a = rotated(send, CHIP, FIRST_CHIP)
    lhs, sd, peak, phi, nd, v_own = own_block(at, doc_lengths, queries, kv_own, fq_weight, fk_weight)
    a, lhs = lax.optimization_barrier((a, lhs))
    b = lax.ppermute(a, CORE, [(0, 1), (1, 0)])
    sa, max_a, state_a = same_core(at, doc_lengths, a, lhs, heads)
    residual, loss = other_core(
        at, doc_lengths, a, b, lhs, sa, max_a, state_a, sd, peak, phi, nd, v_own, lax.axis_size("head")
    )
    parts = rotated(loss, "head", FIRST_PLANE)
    return residual, jnp.sum(parts, axis=0)


def solution(mesh):
    split = Mesh(mesh.devices.reshape(4, 4, 2, mesh.shape["head"]), (*SEQ, "head"))
    placed = (
        P(SEQ, "head"),
        P(SEQ, None),
        P(SEQ, None),
        P(),
        P("head", None, None),
        P("head", None, None),
    )
    return jax.shard_map(
        body, mesh=split, in_specs=placed, out_specs=(P(SEQ, "head"), P(SEQ)), check_vma=False
    )
```

```python
import math

import jax
import jax.numpy as jnp
from jax import lax
from jax.experimental import pallas as pl
from jax.experimental.pallas import tpu as pltpu
from jax.sharding import Mesh
from jax.sharding import PartitionSpec as P

MAXDOC = 2048
CHIP = ("seq_0", "seq_1")
CORE = "seq_2"
SEQ = (*CHIP, CORE)
NEG = -1e30
FIRST_CHIP, FIRST_PLANE = 14, 10
LOG2E = math.log2(math.e)


def dot(a, b):
    return jnp.dot(a, b, preferred_element_type=jnp.float32)


def split_dot(a, b):
    high = a.astype(jnp.bfloat16)
    low = (a - high.astype(jnp.float32)).astype(jnp.bfloat16)
    return dot(high, b) + dot(low, b)


def slot(c, chips):
    return lax.rem(jnp.maximum(c, 0) + (chips - FIRST_CHIP), chips)


def doc_start(doc_ref, pos):
    start = jnp.zeros_like(pos)
    at = jnp.int32(0)
    for d in range(doc_ref.shape[0]):
        start = jnp.where(pos >= at, at, start)
        at = at + doc_ref[d]
    return start


def softmaxes(proj, axis):
    p = proj * LOG2E
    up = jnp.exp2(p - jnp.max(p, axis=axis, keepdims=True))
    down = jnp.exp2(jnp.min(p, axis=axis, keepdims=True) - p)
    up = up * (1.0 / jnp.sum(up, axis=axis, keepdims=True))
    down = down * (1.0 / jnp.sum(down, axis=axis, keepdims=True))
    return jnp.concatenate([up.astype(jnp.bfloat16), down.astype(jnp.bfloat16)], axis=axis)


def with_ones(v):
    return jnp.concatenate([v, jnp.ones_like(v)], axis=1)


def own_kernel(at_ref, doc_ref, q_ref, kv_ref, fq_ref, fk_ref, lhs_ref, sd_ref, peak_ref, phi_ref, nd_ref, v_own_ref):
    heads, hd, _ = fq_ref.shape
    rows = q_ref.shape[0]
    anchor = (2 * at_ref[0] + at_ref[1]) * rows
    q_pos = anchor + lax.broadcasted_iota(jnp.int32, (rows, 1), 0)
    k_pos = anchor + lax.broadcasted_iota(jnp.int32, (1, rows), 1)
    mask = (k_pos >= doc_start(doc_ref, q_pos)) & (k_pos <= q_pos)
    k_t = kv_ref[:, :rows]
    v = with_ones(kv_ref[:, rows:])
    v_own_ref[...] = v
    for h in range(heads):
        q = q_ref[:, h * hd:(h + 1) * hd]
        lhs_ref[h * rows:(h + 1) * rows, :] = q
        fk_t = jnp.transpose(fk_ref[h].astype(jnp.float32)).astype(jnp.bfloat16)
        lhs_ref[heads * rows + h * hd:heads * rows + (h + 1) * hd, :] = fk_t
        sd = jnp.where(mask, dot(q, k_t) * (hd ** -0.5 * LOG2E), NEG)
        sd_ref[h] = sd
        peak_ref[h] = jnp.broadcast_to(jnp.max(sd, axis=1, keepdims=True), sd.shape)
        phi_q = softmaxes(dot(q, fq_ref[h]), 1)
        phi_ref[h] = phi_q
        phi_k = softmaxes(dot(fk_t, k_t), 0)
        affinity = jnp.where(mask, dot(phi_q, phi_k), 0.0)
        nd_ref[h] = split_dot(affinity, v)


def scan_keys(kv_ref, lhs_ref, s_ref, max_ref, state_ref, c0, parity, first, anchor, before):
    heads, rows, hd = state_ref.shape[0], max_ref.shape[1], kv_ref.shape[1]
    qr = heads * rows
    scale = hd ** -0.5 * LOG2E

    def visible(c, shape, dim):
        lane = lax.broadcasted_iota(jnp.int32, shape, dim)
        pos = (2 * c + parity) * rows + lane + jnp.where(lane < rows, 0, rows)
        return (pos >= first) & (pos < anchor)

    for i in range(s_ref.shape[0]):
        c = c0 + 2 * i
        low, high = slot(c, kv_ref.shape[0]), slot(c + 1, kv_ref.shape[0])
        k_t = jnp.concatenate([kv_ref[low, :, :hd], kv_ref[high, :, :hd]], axis=1)
        v = jnp.concatenate([kv_ref[low, :, hd:], kv_ref[high, :, hd:]], axis=0)
        z = dot(lhs_ref[...], k_t)
        s = jnp.where(visible(c, (1, 2 * rows), 1), z[:qr] * scale, NEG)
        s_ref[i] = s
        m = jnp.maximum(s[:, :rows], s[:, rows:])
        if i > 0:
            m = jnp.maximum(max_ref[...], m)
        elif before is not None:
            m = jnp.maximum(before[0][...], m)
        max_ref[...] = m
        v = with_ones(v) * jnp.where(visible(c, (2 * rows, 1), 0), 1.0, 0.0).astype(jnp.bfloat16)
        for h in range(heads):
            d = dot(softmaxes(z[qr + h * hd:qr + (h + 1) * hd], 0), v)
            if i > 0:
                d = state_ref[h] + d
            elif before is not None:
                d = before[1][h] + d
            state_ref[h] = d


def same_core_kernel(at_ref, doc_ref, a_ref, lhs_ref, s_ref, max_ref, state_ref):
    rows = max_ref.shape[1]
    chip, core = at_ref[0], at_ref[1]
    anchor = (2 * chip + core) * rows
    first = doc_start(doc_ref, anchor)
    scan_keys(a_ref, lhs_ref, s_ref, max_ref, state_ref, chip - 2 * s_ref.shape[0], core, first, anchor, None)


def other_core_kernel(
    at_ref, doc_ref, a_ref, b_ref, lhs_ref, sa_ref, max_a_ref, state_a_ref, sd_ref, peak_ref, phi_ref, nd_ref, v_own_ref,
    res_ref, loss_ref, sb_ref, max_ref, state_ref, acc_ref,
):
    heads, rows, hd = sd_ref.shape
    chip, core = at_ref[0], at_ref[1]
    anchor = (2 * chip + core) * rows
    first = doc_start(doc_ref, anchor)
    steps = sb_ref.shape[0]
    a0, b0 = chip - 2 * steps, chip - 2 * steps + core
    scan_keys(b_ref, lhs_ref, sb_ref, max_ref, state_ref, b0, 1 - core, first, anchor, (max_a_ref, state_a_ref))

    q_pos = anchor + lax.broadcasted_iota(jnp.int32, (rows, 1), 0)
    carried = jnp.broadcast_to(jnp.where(doc_start(doc_ref, q_pos) == first, 1.0, 0.0), (rows, hd)) > 0.5
    for h in range(heads):
        at = slice(h * rows, (h + 1) * rows)
        sd = sd_ref[h]
        off = jnp.broadcast_to(jnp.max(max_ref[at], axis=1, keepdims=True), (rows, hd))
        peak = jnp.maximum(peak_ref[h], jnp.where(carried, off, NEG))
        acc_ref[at] = dot(jnp.exp2(sd - peak).astype(jnp.bfloat16), v_own_ref[...])
        max_ref[at] = jnp.where(carried, peak, -NEG)

    weights, seen = [], []
    for kv_ref, s_ref, c0 in ((a_ref, sa_ref, a0), (b_ref, sb_ref, b0)):
        for i in range(steps):
            c = c0 + 2 * i
            low, high = slot(c, kv_ref.shape[0]), slot(c + 1, kv_ref.shape[0])
            peak = max_ref[...]
            s = s_ref[i]
            weights.append(jnp.exp2(s[:, :rows] - peak).astype(jnp.bfloat16))
            weights.append(jnp.exp2(s[:, rows:] - peak).astype(jnp.bfloat16))
            seen.append(with_ones(kv_ref[low, :, hd:]))
            seen.append(with_ones(kv_ref[high, :, hd:]))
    acc_ref[...] += dot(jnp.concatenate(weights, axis=1), jnp.concatenate(seen, axis=0))

    squares = jnp.zeros((rows, hd), jnp.float32)
    for h in range(heads):
        acc = acc_ref[h * rows:(h + 1) * rows]
        state = state_ref[h]
        high = state.astype(jnp.bfloat16)
        low = (state - high.astype(jnp.float32)).astype(jnp.bfloat16)
        phi = phi_ref[h]
        nd = dot(phi, high) + dot(phi, low)
        own = nd_ref[h]
        numer = own[:, :hd] + jnp.where(carried, nd[:, :hd], 0.0)
        denom = own[:, hd:] + jnp.where(carried, nd[:, hd:], 0.0)
        residual = acc[:, :hd] / acc[:, hd:] - numer / denom
        res_ref[:, h * hd:(h + 1) * hd] = residual
        squares = squares + residual * residual
    loss = jnp.sum(jnp.transpose(squares), axis=0, keepdims=True) * (1.0 / hd)
    loss_ref[...] = jnp.broadcast_to(loss, loss_ref.shape)


F32, BF16 = jnp.float32, jnp.bfloat16
SMEM = pl.BlockSpec(memory_space=pltpu.SMEM)
VMEM = pl.BlockSpec(memory_space=pltpu.VMEM)


def rotated(array, axis, first):
    size = lax.axis_size(axis)
    group = [(first + j) % size for j in range(size)]
    return lax.all_to_all(array, axis, 0, 0, tiled=True, axis_index_groups=[group])


def shapes(*items):
    return tuple(jax.ShapeDtypeStruct(s, t) for s, t in items)


def params(mib):
    return pltpu.CompilerParams(vmem_limit_bytes=mib * 1024 * 1024)


def own_block(at, doc_lengths, queries, kv_own, fq_weight, fk_weight):
    rows = queries.shape[0]
    heads, hd, _ = fq_weight.shape
    return pl.pallas_call(
        own_kernel,
        out_shape=shapes(
            ((heads * (rows + hd), hd), BF16),
            ((heads, rows, rows), F32),
            ((heads, rows, rows), F32),
            ((heads, rows, 2 * hd), BF16),
            ((heads, rows, 2 * hd), F32),
            ((rows, 2 * hd), BF16),
        ),
        in_specs=[SMEM, SMEM] + [VMEM] * 4,
        out_specs=(VMEM,) * 6,
        compiler_params=params(16),
        cost_estimate=pl.CostEstimate(flops=10**9, bytes_accessed=2 * 10**6, transcendentals=10**6),
        name="own_block",
    )(at, doc_lengths, queries, kv_own, fq_weight, fk_weight)


def same_core(at, doc_lengths, a, lhs, heads):
    rows = hd = lhs.shape[1]
    steps = MAXDOC // (4 * rows)
    return pl.pallas_call(
        same_core_kernel,
        out_shape=shapes(
            ((steps, heads * rows, 2 * rows), F32), ((heads * rows, rows), F32), ((heads, 2 * hd, 2 * hd), F32)
        ),
        in_specs=[SMEM, SMEM, VMEM, VMEM],
        out_specs=(VMEM,) * 3,
        compiler_params=params(16),
        cost_estimate=pl.CostEstimate(flops=2 * 10**9, bytes_accessed=4 * 10**6, transcendentals=2 * 10**6),
        name="same_core",
    )(at, doc_lengths, a, lhs)


def other_core(at, doc_lengths, a, b, lhs, sa, max_a, state_a, sd, peak, phi, nd, v_own, planes):
    heads, rows, hd = sd.shape
    return pl.pallas_call(
        other_core_kernel,
        out_shape=shapes(((rows, heads * hd), F32), ((planes, rows), F32)),
        in_specs=[SMEM, SMEM] + [VMEM] * 11,
        out_specs=(VMEM, VMEM),
        scratch_shapes=[
            pltpu.VMEM(sa.shape, F32),
            pltpu.VMEM(max_a.shape, F32),
            pltpu.VMEM(state_a.shape, F32),
            pltpu.VMEM((heads * rows, 2 * hd), F32),
        ],
        compiler_params=params(24),
        cost_estimate=pl.CostEstimate(flops=4 * 10**9, bytes_accessed=4 * 10**6, transcendentals=4 * 10**6),
        name="other_core",
    )(at, doc_lengths, a, b, lhs, sa, max_a, state_a, sd, peak, phi, nd, v_own)


def body(queries, keys, values, doc_lengths, fq_weight, fk_weight):
    heads, hd, _ = fq_weight.shape
    at = jnp.stack([lax.axis_index(CHIP), lax.axis_index(CORE)]).astype(jnp.int32)
    kv_head = lax.axis_index("head") * (keys.shape[1] // hd) // lax.axis_size("head")
    k_own = lax.dynamic_slice_in_dim(keys, kv_head * hd, hd, 1)
    v_own = lax.dynamic_slice_in_dim(values, kv_head * hd, hd, 1)
    kv_own = jnp.concatenate([k_own.T, v_own], axis=1)
    send = jnp.broadcast_to(kv_own, (lax.axis_size(CHIP), *kv_own.shape))
    a = rotated(send, CHIP, FIRST_CHIP)
    lhs, sd, peak, phi, nd, v_own = own_block(at, doc_lengths, queries, kv_own, fq_weight, fk_weight)
    a, lhs = lax.optimization_barrier((a, lhs))
    b = lax.ppermute(a, CORE, [(0, 1), (1, 0)])
    sa, max_a, state_a = same_core(at, doc_lengths, a, lhs, heads)
    residual, loss = other_core(
        at, doc_lengths, a, b, lhs, sa, max_a, state_a, sd, peak, phi, nd, v_own, lax.axis_size("head")
    )
    parts = rotated(loss, "head", FIRST_PLANE)
    return residual, jnp.sum(parts, axis=0)


def solution(mesh):
    split = Mesh(mesh.devices.reshape(4, 4, 2, mesh.shape["head"]), (*SEQ, "head"))
    placed = (
        P(SEQ, "head"),
        P(SEQ, None),
        P(SEQ, None),
        P(),
        P("head", None, None),
        P("head", None, None),
    )
    return jax.shard_map(
        body, mesh=split, in_specs=placed, out_specs=(P(SEQ, "head"), P(SEQ)), check_vma=False
    )
```

```python
import functools
import math

import jax
import jax.numpy as jnp
from jax import lax
from jax.experimental import pallas as pl
from jax.experimental.pallas import tpu as pltpu
from jax.sharding import Mesh
from jax.sharding import PartitionSpec as P

MAXDOC = 2048
CHIP = ("seq_0", "seq_1")
CORE = "seq_2"
SEQ = (*CHIP, CORE)
NEG = -1e30
FIRST_CHIP, FIRST_PLANE = 14, 10
LOG2E = math.log2(math.e)


def dot(a, b):
    return jnp.dot(a, b, preferred_element_type=jnp.float32)


def split_dot(a, b):
    high = a.astype(jnp.bfloat16)
    low = (a - high.astype(jnp.float32)).astype(jnp.bfloat16)
    return dot(high, b) + dot(low, b)


def slot(c, chips):
    return lax.rem(jnp.maximum(c, 0) + (chips - FIRST_CHIP), chips)


def doc_start(doc_ref, pos):
    start = jnp.zeros_like(pos)
    at = jnp.int32(0)
    for d in range(doc_ref.shape[0]):
        start = jnp.where(pos >= at, at, start)
        at = at + doc_ref[d]
    return start


def softmaxes(proj, axis):
    p = proj * LOG2E
    up = jnp.exp2(p - jnp.max(p, axis=axis, keepdims=True))
    down = jnp.exp2(jnp.min(p, axis=axis, keepdims=True) - p)
    up = up * (1.0 / jnp.sum(up, axis=axis, keepdims=True))
    down = down * (1.0 / jnp.sum(down, axis=axis, keepdims=True))
    return jnp.concatenate([up.astype(jnp.bfloat16), down.astype(jnp.bfloat16)], axis=axis)


def with_ones(v):
    return jnp.concatenate([v, jnp.ones_like(v)], axis=1)


def own_kernel(at_ref, doc_ref, q_ref, kv_ref, fq_ref, fk_ref, lhs_ref, sd_ref, peak_ref, phi_ref, nd_ref, v_own_ref):
    heads, hd, _ = fq_ref.shape
    rows = q_ref.shape[0]
    anchor = (2 * at_ref[0] + at_ref[1]) * rows
    q_pos = anchor + lax.broadcasted_iota(jnp.int32, (rows, 1), 0)
    k_pos = anchor + lax.broadcasted_iota(jnp.int32, (1, rows), 1)
    mask = (k_pos >= doc_start(doc_ref, q_pos)) & (k_pos <= q_pos)
    k_t = kv_ref[:, :rows]
    v = with_ones(kv_ref[:, rows:])
    v_own_ref[...] = v
    for h in range(heads):
        q = q_ref[:, h * hd:(h + 1) * hd]
        lhs_ref[h * rows:(h + 1) * rows, :] = q
        fk_t = jnp.transpose(fk_ref[h].astype(jnp.float32)).astype(jnp.bfloat16)
        lhs_ref[heads * rows + h * hd:heads * rows + (h + 1) * hd, :] = fk_t
        sd = jnp.where(mask, dot(q, k_t) * (hd ** -0.5 * LOG2E), NEG)
        sd_ref[h] = sd
        peak_ref[h] = jnp.broadcast_to(jnp.max(sd, axis=1, keepdims=True), sd.shape)
        phi_q = softmaxes(dot(q, fq_ref[h]), 1)
        phi_ref[h] = phi_q
        phi_k = softmaxes(dot(fk_t, k_t), 0)
        affinity = jnp.where(mask, dot(phi_q, phi_k), 0.0)
        nd_ref[h] = split_dot(affinity, v)


def scan_keys(kv_ref, lhs_ref, s_ref, max_ref, state_ref, c0, parity, first, anchor, before, skip):
    heads, rows, hd = state_ref.shape[0], max_ref.shape[1], kv_ref.shape[1]
    qr = heads * rows
    scale = hd ** -0.5 * LOG2E

    def visible(c, shape, dim):
        lane = lax.broadcasted_iota(jnp.int32, shape, dim)
        pos = (2 * c + parity) * rows + lane + jnp.where(lane < rows, 0, rows)
        return (pos >= first) & (pos < anchor)

    for i in range(skip, s_ref.shape[0]):
        c = c0 + 2 * i
        low, high = slot(c, kv_ref.shape[0]), slot(c + 1, kv_ref.shape[0])
        k_t = jnp.concatenate([kv_ref[low, :, :hd], kv_ref[high, :, :hd]], axis=1)
        v = jnp.concatenate([kv_ref[low, :, hd:], kv_ref[high, :, hd:]], axis=0)
        z = dot(lhs_ref[...], k_t)
        s = jnp.where(visible(c, (1, 2 * rows), 1), z[:qr] * scale, NEG)
        s_ref[i] = s
        m = jnp.maximum(s[:, :rows], s[:, rows:])
        if i > skip:
            m = jnp.maximum(max_ref[...], m)
        elif before is not None:
            m = jnp.maximum(before[0][...], m)
        max_ref[...] = m
        v = with_ones(v) * jnp.where(visible(c, (2 * rows, 1), 0), 1.0, 0.0).astype(jnp.bfloat16)
        for h in range(heads):
            d = dot(softmaxes(z[qr + h * hd:qr + (h + 1) * hd], 0), v)
            if i > skip:
                d = state_ref[h] + d
            elif before is not None:
                d = before[1][h] + d
            state_ref[h] = d


def as_far_as_needed(first, anchor, rows, steps, run):
    skips = (steps - 1, steps // 2, 0)
    nearer = False
    for skip in skips:
        reached = first >= anchor - 4 * (steps - skip) * rows if skip else True
        pl.when(jnp.logical_and(reached, jnp.logical_not(nearer)))(functools.partial(run, skip))
        nearer = jnp.logical_or(nearer, reached)


def same_core_kernel(at_ref, doc_ref, a_ref, lhs_ref, s_ref, max_ref, state_ref):
    rows = max_ref.shape[1]
    chip, core = at_ref[0], at_ref[1]
    anchor = (2 * chip + core) * rows
    first = doc_start(doc_ref, anchor)
    steps = s_ref.shape[0]

    def run(skip):
        scan_keys(a_ref, lhs_ref, s_ref, max_ref, state_ref, chip - 2 * steps, core, first, anchor, None, skip)

    as_far_as_needed(first, anchor, rows, steps, run)


def other_core_kernel(
    at_ref, doc_ref, a_ref, b_ref, lhs_ref, sa_ref, max_a_ref, state_a_ref, sd_ref, peak_ref, phi_ref, nd_ref, v_own_ref,
    res_ref, loss_ref, sb_ref, max_ref, state_ref, acc_ref,
):
    heads, rows, hd = sd_ref.shape
    chip, core = at_ref[0], at_ref[1]
    anchor = (2 * chip + core) * rows
    first = doc_start(doc_ref, anchor)
    steps = sb_ref.shape[0]
    a0, b0 = chip - 2 * steps, chip - 2 * steps + core
    q_pos = anchor + lax.broadcasted_iota(jnp.int32, (rows, 1), 0)
    carried = jnp.broadcast_to(jnp.where(doc_start(doc_ref, q_pos) == first, 1.0, 0.0), (rows, hd)) > 0.5

    def run(skip):
        before = (max_a_ref, state_a_ref)
        scan_keys(b_ref, lhs_ref, sb_ref, max_ref, state_ref, b0, 1 - core, first, anchor, before, skip)
        for h in range(heads):
            at = slice(h * rows, (h + 1) * rows)
            off = jnp.broadcast_to(jnp.max(max_ref[at], axis=1, keepdims=True), (rows, hd))
            peak = jnp.maximum(peak_ref[h], jnp.where(carried, off, NEG))
            acc_ref[at] = dot(jnp.exp2(sd_ref[h] - peak).astype(jnp.bfloat16), v_own_ref[...])
            max_ref[at] = jnp.where(carried, peak, -NEG)

        weights, seen = [], []
        for kv_ref, s_ref, c0 in ((a_ref, sa_ref, a0), (b_ref, sb_ref, b0)):
            for i in range(skip, steps):
                c = c0 + 2 * i
                low, high = slot(c, kv_ref.shape[0]), slot(c + 1, kv_ref.shape[0])
                peak = max_ref[...]
                s = s_ref[i]
                weights.append(jnp.exp2(s[:, :rows] - peak).astype(jnp.bfloat16))
                weights.append(jnp.exp2(s[:, rows:] - peak).astype(jnp.bfloat16))
                seen.append(with_ones(kv_ref[low, :, hd:]))
                seen.append(with_ones(kv_ref[high, :, hd:]))
        acc_ref[...] += dot(jnp.concatenate(weights, axis=1), jnp.concatenate(seen, axis=0))

    as_far_as_needed(first, anchor, rows, steps, run)

    squares = jnp.zeros((rows, hd), jnp.float32)
    for h in range(heads):
        acc = acc_ref[h * rows:(h + 1) * rows]
        state = state_ref[h]
        high = state.astype(jnp.bfloat16)
        low = (state - high.astype(jnp.float32)).astype(jnp.bfloat16)
        phi = phi_ref[h]
        nd = dot(phi, high) + dot(phi, low)
        own = nd_ref[h]
        numer = own[:, :hd] + jnp.where(carried, nd[:, :hd], 0.0)
        denom = own[:, hd:] + jnp.where(carried, nd[:, hd:], 0.0)
        residual = acc[:, :hd] / acc[:, hd:] - numer / denom
        res_ref[:, h * hd:(h + 1) * hd] = residual
        squares = squares + residual * residual
    loss = jnp.sum(jnp.transpose(squares), axis=0, keepdims=True) * (1.0 / hd)
    loss_ref[...] = jnp.broadcast_to(loss, loss_ref.shape)


F32, BF16 = jnp.float32, jnp.bfloat16
SMEM = pl.BlockSpec(memory_space=pltpu.SMEM)
VMEM = pl.BlockSpec(memory_space=pltpu.VMEM)


def rotated(array, axis, first):
    size = lax.axis_size(axis)
    group = [(first + j) % size for j in range(size)]
    return lax.all_to_all(array, axis, 0, 0, tiled=True, axis_index_groups=[group])


def shapes(*items):
    return tuple(jax.ShapeDtypeStruct(s, t) for s, t in items)


def params(mib):
    return pltpu.CompilerParams(vmem_limit_bytes=mib * 1024 * 1024)


def own_block(at, doc_lengths, queries, kv_own, fq_weight, fk_weight):
    rows = queries.shape[0]
    heads, hd, _ = fq_weight.shape
    return pl.pallas_call(
        own_kernel,
        out_shape=shapes(
            ((heads * (rows + hd), hd), BF16),
            ((heads, rows, rows), F32),
            ((heads, rows, rows), F32),
            ((heads, rows, 2 * hd), BF16),
            ((heads, rows, 2 * hd), F32),
            ((rows, 2 * hd), BF16),
        ),
        in_specs=[SMEM, SMEM] + [VMEM] * 4,
        out_specs=(VMEM,) * 6,
        compiler_params=params(16),
        cost_estimate=pl.CostEstimate(flops=10**9, bytes_accessed=2 * 10**6, transcendentals=10**6),
        name="own_block",
    )(at, doc_lengths, queries, kv_own, fq_weight, fk_weight)


def same_core(at, doc_lengths, a, lhs, heads):
    rows = hd = lhs.shape[1]
    steps = MAXDOC // (4 * rows)
    return pl.pallas_call(
        same_core_kernel,
        out_shape=shapes(
            ((steps, heads * rows, 2 * rows), F32), ((heads * rows, rows), F32), ((heads, 2 * hd, 2 * hd), F32)
        ),
        in_specs=[SMEM, SMEM, VMEM, VMEM],
        out_specs=(VMEM,) * 3,
        compiler_params=params(16),
        cost_estimate=pl.CostEstimate(flops=2 * 10**9, bytes_accessed=4 * 10**6, transcendentals=2 * 10**6),
        name="same_core",
    )(at, doc_lengths, a, lhs)


def other_core(at, doc_lengths, a, b, lhs, sa, max_a, state_a, sd, peak, phi, nd, v_own, planes):
    heads, rows, hd = sd.shape
    return pl.pallas_call(
        other_core_kernel,
        out_shape=shapes(((rows, heads * hd), F32), ((planes, rows), F32)),
        in_specs=[SMEM, SMEM] + [VMEM] * 11,
        out_specs=(VMEM, VMEM),
        scratch_shapes=[
            pltpu.VMEM(sa.shape, F32),
            pltpu.VMEM(max_a.shape, F32),
            pltpu.VMEM(state_a.shape, F32),
            pltpu.VMEM((heads * rows, 2 * hd), F32),
        ],
        compiler_params=params(24),
        cost_estimate=pl.CostEstimate(flops=4 * 10**9, bytes_accessed=4 * 10**6, transcendentals=4 * 10**6),
        name="other_core",
    )(at, doc_lengths, a, b, lhs, sa, max_a, state_a, sd, peak, phi, nd, v_own)


def body(queries, keys, values, doc_lengths, fq_weight, fk_weight):
    heads, hd, _ = fq_weight.shape
    at = jnp.stack([lax.axis_index(CHIP), lax.axis_index(CORE)]).astype(jnp.int32)
    kv_head = lax.axis_index("head") * (keys.shape[1] // hd) // lax.axis_size("head")
    k_own = lax.dynamic_slice_in_dim(keys, kv_head * hd, hd, 1)
    v_own = lax.dynamic_slice_in_dim(values, kv_head * hd, hd, 1)
    kv_own = jnp.concatenate([k_own.T, v_own], axis=1)
    send = jnp.broadcast_to(kv_own, (lax.axis_size(CHIP), *kv_own.shape))
    a = rotated(send, CHIP, FIRST_CHIP)
    lhs, sd, peak, phi, nd, v_own = own_block(at, doc_lengths, queries, kv_own, fq_weight, fk_weight)
    a, lhs = lax.optimization_barrier((a, lhs))
    b = lax.ppermute(a, CORE, [(0, 1), (1, 0)])
    sa, max_a, state_a = same_core(at, doc_lengths, a, lhs, heads)
    residual, loss = other_core(
        at, doc_lengths, a, b, lhs, sa, max_a, state_a, sd, peak, phi, nd, v_own, lax.axis_size("head")
    )
    parts = rotated(loss, "head", FIRST_PLANE)
    return residual, jnp.sum(parts, axis=0)


def solution(mesh):
    split = Mesh(mesh.devices.reshape(4, 4, 2, mesh.shape["head"]), (*SEQ, "head"))
    placed = (
        P(SEQ, "head"),
        P(SEQ, None),
        P(SEQ, None),
        P(),
        P("head", None, None),
        P("head", None, None),
    )
    return jax.shard_map(
        body, mesh=split, in_specs=placed, out_specs=(P(SEQ, "head"), P(SEQ)), check_vma=False
    )
```

```python
import functools
import math

import jax
import jax.numpy as jnp
from jax import lax
from jax.experimental import pallas as pl
from jax.experimental.pallas import tpu as pltpu
from jax.sharding import Mesh
from jax.sharding import PartitionSpec as P

MAXDOC = 2048
CHIP = ("seq_0", "seq_1")
CORE = "seq_2"
SEQ = (*CHIP, CORE)
NEG = -1e30
MOST_KEY = 6.0
LIMIT = 115.0
FIRST_CHIP, FIRST_PLANE = 14, 10
LOG2E = math.log2(math.e)


def dot(a, b):
    return jnp.dot(a, b, preferred_element_type=jnp.float32)


def split_dot(a, b):
    high = a.astype(jnp.bfloat16)
    low = (a - high.astype(jnp.float32)).astype(jnp.bfloat16)
    return dot(high, b) + dot(low, b)


def slot(c, chips):
    return lax.rem(jnp.maximum(c, 0) + (chips - FIRST_CHIP), chips)


def doc_start(doc_ref, pos):
    start = jnp.zeros_like(pos)
    at = jnp.int32(0)
    for d in range(doc_ref.shape[0]):
        start = jnp.where(pos >= at, at, start)
        at = at + doc_ref[d]
    return start


def softmaxes(proj, axis, small=False):
    p = proj * LOG2E
    if small:
        up, down = jnp.exp2(p), jnp.exp2(-p)
    else:
        up = jnp.exp2(p - jnp.max(p, axis=axis, keepdims=True))
        down = jnp.exp2(jnp.min(p, axis=axis, keepdims=True) - p)
    up = up * (1.0 / jnp.sum(up, axis=axis, keepdims=True))
    down = down * (1.0 / jnp.sum(down, axis=axis, keepdims=True))
    return jnp.concatenate([up.astype(jnp.bfloat16), down.astype(jnp.bfloat16)], axis=axis)


def with_ones(v):
    return jnp.concatenate([v, jnp.ones_like(v)], axis=1)


def own_kernel(at_ref, doc_ref, q_ref, kv_ref, fq_ref, fk_ref, lhs_ref, sd_ref, peak_ref, phi_ref, nd_ref, v_own_ref, most_ref):
    heads, hd, _ = fq_ref.shape
    rows = q_ref.shape[0]
    anchor = (2 * at_ref[0] + at_ref[1]) * rows
    q_pos = anchor + lax.broadcasted_iota(jnp.int32, (rows, 1), 0)
    k_pos = anchor + lax.broadcasted_iota(jnp.int32, (1, rows), 1)
    mask = (k_pos >= doc_start(doc_ref, q_pos)) & (k_pos <= q_pos)
    k_t = kv_ref[:, :rows]
    v = with_ones(kv_ref[:, rows:])
    v_own_ref[...] = v
    most = jnp.zeros((hd, 1), jnp.float32)
    for h in range(heads):
        q = q_ref[:, h * hd:(h + 1) * hd]
        lhs_ref[h * rows:(h + 1) * rows, :] = q
        fk_t = jnp.transpose(fk_ref[h].astype(jnp.float32))
        most = jnp.maximum(most, jnp.sum(jnp.abs(fk_t), axis=1, keepdims=True))
        fk_t = fk_t.astype(jnp.bfloat16)
        lhs_ref[heads * rows + h * hd:heads * rows + (h + 1) * hd, :] = fk_t
        sd = jnp.where(mask, dot(q, k_t) * (hd ** -0.5 * LOG2E), NEG)
        sd_ref[h] = sd
        peak_ref[h] = jnp.broadcast_to(jnp.max(sd, axis=1, keepdims=True), sd.shape)
        phi_q = softmaxes(dot(q, fq_ref[h]), 1)
        phi_ref[h] = phi_q
        phi_k = softmaxes(dot(fk_t, k_t), 0)
        affinity = jnp.where(mask, dot(phi_q, phi_k), 0.0)
        nd_ref[h] = split_dot(affinity, v)
    most_ref[...] = jnp.full(most_ref.shape, jnp.max(most) * (MOST_KEY * LOG2E), jnp.float32)


def scan_keys(kv_ref, lhs_ref, s_ref, max_ref, state_ref, c0, parity, first, anchor, before, skip, small):
    heads, rows, hd = state_ref.shape[0], max_ref.shape[1], kv_ref.shape[1]
    qr = heads * rows
    scale = hd ** -0.5 * LOG2E

    def visible(c, shape, dim):
        lane = lax.broadcasted_iota(jnp.int32, shape, dim)
        pos = (2 * c + parity) * rows + lane + jnp.where(lane < rows, 0, rows)
        return (pos >= first) & (pos < anchor)

    for i in range(skip, s_ref.shape[0]):
        c = c0 + 2 * i
        low, high = slot(c, kv_ref.shape[0]), slot(c + 1, kv_ref.shape[0])
        k_t = jnp.concatenate([kv_ref[low, :, :hd], kv_ref[high, :, :hd]], axis=1)
        v = jnp.concatenate([kv_ref[low, :, hd:], kv_ref[high, :, hd:]], axis=0)
        z = dot(lhs_ref[...], k_t)
        s = jnp.where(visible(c, (1, 2 * rows), 1), z[:qr] * scale, NEG)
        s_ref[i] = s
        m = jnp.maximum(s[:, :rows], s[:, rows:])
        if i > skip:
            m = jnp.maximum(max_ref[...], m)
        elif before is not None:
            m = jnp.maximum(before[0][...], m)
        max_ref[...] = m
        v = with_ones(v) * jnp.where(visible(c, (2 * rows, 1), 0), 1.0, 0.0).astype(jnp.bfloat16)
        for h in range(heads):
            d = dot(softmaxes(z[qr + h * hd:qr + (h + 1) * hd], 0, small), v)
            if i > skip:
                d = state_ref[h] + d
            elif before is not None:
                d = before[1][h] + d
            state_ref[h] = d


def as_far_as_needed(first, anchor, rows, steps, most, run):
    small = most <= LIMIT
    pl.when(jnp.logical_not(small))(functools.partial(run, 0, False))
    left = small
    for skip in (steps - 1, steps // 2, 0):
        reached = first >= anchor - 4 * (steps - skip) * rows if skip else True
        pl.when(jnp.logical_and(left, reached))(functools.partial(run, skip, True))
        left = jnp.logical_and(left, jnp.logical_not(reached))


def same_core_kernel(at_ref, doc_ref, most_ref, a_ref, lhs_ref, s_ref, max_ref, state_ref):
    rows = max_ref.shape[1]
    chip, core = at_ref[0], at_ref[1]
    anchor = (2 * chip + core) * rows
    first = doc_start(doc_ref, anchor)
    steps = s_ref.shape[0]

    def run(skip, small):
        scan_keys(a_ref, lhs_ref, s_ref, max_ref, state_ref, chip - 2 * steps, core, first, anchor, None, skip, small)

    as_far_as_needed(first, anchor, rows, steps, jnp.max(most_ref[0:1, 0:1]), run)


def other_core_kernel(
    at_ref, doc_ref, most_ref, a_ref, b_ref, lhs_ref, sa_ref, max_a_ref, state_a_ref, sd_ref, peak_ref, phi_ref, nd_ref, v_own_ref,
    res_ref, loss_ref, sb_ref, max_ref, state_ref, acc_ref,
):
    heads, rows, hd = sd_ref.shape
    chip, core = at_ref[0], at_ref[1]
    anchor = (2 * chip + core) * rows
    first = doc_start(doc_ref, anchor)
    steps = sb_ref.shape[0]
    a0, b0 = chip - 2 * steps, chip - 2 * steps + core
    q_pos = anchor + lax.broadcasted_iota(jnp.int32, (rows, 1), 0)
    carried = jnp.broadcast_to(jnp.where(doc_start(doc_ref, q_pos) == first, 1.0, 0.0), (rows, hd)) > 0.5

    def run(skip, small):
        before = (max_a_ref, state_a_ref)
        scan_keys(b_ref, lhs_ref, sb_ref, max_ref, state_ref, b0, 1 - core, first, anchor, before, skip, small)
        for h in range(heads):
            at = slice(h * rows, (h + 1) * rows)
            off = jnp.broadcast_to(jnp.max(max_ref[at], axis=1, keepdims=True), (rows, hd))
            peak = jnp.maximum(peak_ref[h], jnp.where(carried, off, NEG))
            acc_ref[at] = dot(jnp.exp2(sd_ref[h] - peak).astype(jnp.bfloat16), v_own_ref[...])
            max_ref[at] = jnp.where(carried, peak, -NEG)

        weights, seen = [], []
        for kv_ref, s_ref, c0 in ((a_ref, sa_ref, a0), (b_ref, sb_ref, b0)):
            for i in range(skip, steps):
                c = c0 + 2 * i
                low, high = slot(c, kv_ref.shape[0]), slot(c + 1, kv_ref.shape[0])
                peak = max_ref[...]
                s = s_ref[i]
                weights.append(jnp.exp2(s[:, :rows] - peak).astype(jnp.bfloat16))
                weights.append(jnp.exp2(s[:, rows:] - peak).astype(jnp.bfloat16))
                seen.append(with_ones(kv_ref[low, :, hd:]))
                seen.append(with_ones(kv_ref[high, :, hd:]))
        acc_ref[...] += dot(jnp.concatenate(weights, axis=1), jnp.concatenate(seen, axis=0))

    as_far_as_needed(first, anchor, rows, steps, jnp.max(most_ref[0:1, 0:1]), run)

    squares = jnp.zeros((rows, hd), jnp.float32)
    for h in range(heads):
        acc = acc_ref[h * rows:(h + 1) * rows]
        state = state_ref[h]
        high = state.astype(jnp.bfloat16)
        low = (state - high.astype(jnp.float32)).astype(jnp.bfloat16)
        phi = phi_ref[h]
        nd = dot(phi, high) + dot(phi, low)
        own = nd_ref[h]
        numer = own[:, :hd] + jnp.where(carried, nd[:, :hd], 0.0)
        denom = own[:, hd:] + jnp.where(carried, nd[:, hd:], 0.0)
        residual = acc[:, :hd] / acc[:, hd:] - numer / denom
        res_ref[:, h * hd:(h + 1) * hd] = residual
        squares = squares + residual * residual
    loss = jnp.sum(jnp.transpose(squares), axis=0, keepdims=True) * (1.0 / hd)
    loss_ref[...] = jnp.broadcast_to(loss, loss_ref.shape)


F32, BF16 = jnp.float32, jnp.bfloat16
SMEM = pl.BlockSpec(memory_space=pltpu.SMEM)
VMEM = pl.BlockSpec(memory_space=pltpu.VMEM)


def rotated(array, axis, first):
    size = lax.axis_size(axis)
    group = [(first + j) % size for j in range(size)]
    return lax.all_to_all(array, axis, 0, 0, tiled=True, axis_index_groups=[group])


def shapes(*items):
    return tuple(jax.ShapeDtypeStruct(s, t) for s, t in items)


def params(mib):
    return pltpu.CompilerParams(vmem_limit_bytes=mib * 1024 * 1024)


def own_block(at, doc_lengths, queries, kv_own, fq_weight, fk_weight):
    rows = queries.shape[0]
    heads, hd, _ = fq_weight.shape
    return pl.pallas_call(
        own_kernel,
        out_shape=shapes(
            ((heads * (rows + hd), hd), BF16),
            ((heads, rows, rows), F32),
            ((heads, rows, rows), F32),
            ((heads, rows, 2 * hd), BF16),
            ((heads, rows, 2 * hd), F32),
            ((rows, 2 * hd), BF16),
            ((8, 128), F32),
        ),
        in_specs=[SMEM, SMEM] + [VMEM] * 4,
        out_specs=(VMEM,) * 7,
        compiler_params=params(16),
        cost_estimate=pl.CostEstimate(flops=10**9, bytes_accessed=2 * 10**6, transcendentals=10**6),
        name="own_block",
    )(at, doc_lengths, queries, kv_own, fq_weight, fk_weight)


def same_core(at, doc_lengths, most, a, lhs, heads):
    rows = hd = lhs.shape[1]
    steps = MAXDOC // (4 * rows)
    return pl.pallas_call(
        same_core_kernel,
        out_shape=shapes(
            ((steps, heads * rows, 2 * rows), F32), ((heads * rows, rows), F32), ((heads, 2 * hd, 2 * hd), F32)
        ),
        in_specs=[SMEM, SMEM, VMEM, VMEM, VMEM],
        out_specs=(VMEM,) * 3,
        compiler_params=params(16),
        cost_estimate=pl.CostEstimate(flops=2 * 10**9, bytes_accessed=4 * 10**6, transcendentals=2 * 10**6),
        name="same_core",
    )(at, doc_lengths, most, a, lhs)


def other_core(at, doc_lengths, most, a, b, lhs, sa, max_a, state_a, sd, peak, phi, nd, v_own, planes):
    heads, rows, hd = sd.shape
    return pl.pallas_call(
        other_core_kernel,
        out_shape=shapes(((rows, heads * hd), F32), ((planes, rows), F32)),
        in_specs=[SMEM] * 2 + [VMEM] * 12,
        out_specs=(VMEM, VMEM),
        scratch_shapes=[
            pltpu.VMEM(sa.shape, F32),
            pltpu.VMEM(max_a.shape, F32),
            pltpu.VMEM(state_a.shape, F32),
            pltpu.VMEM((heads * rows, 2 * hd), F32),
        ],
        compiler_params=params(24),
        cost_estimate=pl.CostEstimate(flops=4 * 10**9, bytes_accessed=4 * 10**6, transcendentals=4 * 10**6),
        name="other_core",
    )(at, doc_lengths, most, a, b, lhs, sa, max_a, state_a, sd, peak, phi, nd, v_own)


def body(queries, keys, values, doc_lengths, fq_weight, fk_weight):
    heads, hd, _ = fq_weight.shape
    at = jnp.stack([lax.axis_index(CHIP), lax.axis_index(CORE)]).astype(jnp.int32)
    kv_head = lax.axis_index("head") * (keys.shape[1] // hd) // lax.axis_size("head")
    k_own = lax.dynamic_slice_in_dim(keys, kv_head * hd, hd, 1)
    v_own = lax.dynamic_slice_in_dim(values, kv_head * hd, hd, 1)
    kv_own = jnp.concatenate([k_own.T, v_own], axis=1)
    send = jnp.broadcast_to(kv_own, (lax.axis_size(CHIP), *kv_own.shape))
    a = rotated(send, CHIP, FIRST_CHIP)
    lhs, sd, peak, phi, nd, v_own, most = own_block(at, doc_lengths, queries, kv_own, fq_weight, fk_weight)
    a, lhs = lax.optimization_barrier((a, lhs))
    b = lax.ppermute(a, CORE, [(0, 1), (1, 0)])
    sa, max_a, state_a = same_core(at, doc_lengths, most, a, lhs, heads)
    residual, loss = other_core(
        at, doc_lengths, most, a, b, lhs, sa, max_a, state_a, sd, peak, phi, nd, v_own, lax.axis_size("head")
    )
    parts = rotated(loss, "head", FIRST_PLANE)
    return residual, jnp.sum(parts, axis=0)


def solution(mesh):
    split = Mesh(mesh.devices.reshape(4, 4, 2, mesh.shape["head"]), (*SEQ, "head"))
    placed = (
        P(SEQ, "head"),
        P(SEQ, None),
        P(SEQ, None),
        P(),
        P("head", None, None),
        P("head", None, None),
    )
    return jax.shard_map(
        body, mesh=split, in_specs=placed, out_specs=(P(SEQ, "head"), P(SEQ)), check_vma=False
    )
```

```python
import functools
import math

import jax
import jax.numpy as jnp
from jax import lax
from jax.experimental import pallas as pl
from jax.experimental.pallas import tpu as pltpu
from jax.sharding import Mesh
from jax.sharding import PartitionSpec as P

MAXDOC = 2048
CHIP = ("seq_0", "seq_1")
CORE = "seq_2"
SEQ = (*CHIP, CORE)
NEG = -1e30
MOST_KEY = 6.0
LIMIT = 115.0
FIRST_CHIP, FIRST_PLANE = 14, 10
LOG2E = math.log2(math.e)


def dot(a, b):
    return jnp.dot(a, b, preferred_element_type=jnp.float32)


def split_dot(a, b):
    high = a.astype(jnp.bfloat16)
    low = (a - high.astype(jnp.float32)).astype(jnp.bfloat16)
    return dot(high, b) + dot(low, b)


def slot(c, chips):
    return lax.rem(jnp.maximum(c, 0) + (chips - FIRST_CHIP), chips)


def doc_start(doc_ref, pos):
    start = jnp.zeros_like(pos)
    at = jnp.int32(0)
    for d in range(doc_ref.shape[0]):
        start = jnp.where(pos >= at, at, start)
        at = at + doc_ref[d]
    return start


def softmaxes(proj, axis, small=False):
    p = proj * LOG2E
    if small:
        up, down = jnp.exp2(p), jnp.exp2(-p)
    else:
        up = jnp.exp2(p - jnp.max(p, axis=axis, keepdims=True))
        down = jnp.exp2(jnp.min(p, axis=axis, keepdims=True) - p)
    up = up * (1.0 / jnp.sum(up, axis=axis, keepdims=True))
    down = down * (1.0 / jnp.sum(down, axis=axis, keepdims=True))
    return jnp.concatenate([up.astype(jnp.bfloat16), down.astype(jnp.bfloat16)], axis=axis)


def with_ones(v):
    return jnp.concatenate([v, jnp.ones_like(v)], axis=1)


def own_kernel(at_ref, doc_ref, q_ref, kv_ref, fq_ref, fk_ref, lhs_ref, sd_ref, peak_ref, phi_ref, nd_ref, v_own_ref, most_ref):
    heads, hd, _ = fq_ref.shape
    rows = q_ref.shape[0]
    anchor = (2 * at_ref[0] + at_ref[1]) * rows
    q_pos = anchor + lax.broadcasted_iota(jnp.int32, (rows, 1), 0)
    k_pos = anchor + lax.broadcasted_iota(jnp.int32, (1, rows), 1)
    mask = (k_pos >= doc_start(doc_ref, q_pos)) & (k_pos <= q_pos)
    k_t = kv_ref[:, :rows]
    v = with_ones(kv_ref[:, rows:])
    v_own_ref[...] = v
    most = jnp.zeros((hd, 1), jnp.float32)
    for h in range(heads):
        q = q_ref[:, h * hd:(h + 1) * hd]
        lhs_ref[h * rows:(h + 1) * rows, :] = q
        fk_t = jnp.transpose(fk_ref[h].astype(jnp.float32))
        most = jnp.maximum(most, jnp.sum(jnp.abs(fk_t), axis=1, keepdims=True))
        fk_t = fk_t.astype(jnp.bfloat16)
        lhs_ref[heads * rows + h * hd:heads * rows + (h + 1) * hd, :] = fk_t
        sd = jnp.where(mask, dot(q, k_t) * (hd ** -0.5 * LOG2E), NEG)
        sd_ref[h] = sd
        peak_ref[h] = jnp.broadcast_to(jnp.max(sd, axis=1, keepdims=True), sd.shape)
        phi_q = softmaxes(dot(q, fq_ref[h]), 1)
        phi_ref[h] = phi_q
        phi_k = softmaxes(dot(fk_t, k_t), 0)
        affinity = jnp.where(mask, dot(phi_q, phi_k), 0.0)
        nd_ref[h] = split_dot(affinity, v)
    most_ref[...] = jnp.full(most_ref.shape, jnp.max(most) * (MOST_KEY * LOG2E), jnp.float32)


def scan_keys(kv_ref, lhs_ref, s_ref, max_ref, state_ref, c0, parity, first, anchor, before, skip, small):
    heads, rows, hd = state_ref.shape[0], max_ref.shape[1], kv_ref.shape[1]
    qr = heads * rows
    scale = hd ** -0.5 * LOG2E

    def visible(c, shape, dim):
        lane = lax.broadcasted_iota(jnp.int32, shape, dim)
        pos = (2 * c + parity) * rows + lane + jnp.where(lane < rows, 0, rows)
        return (pos >= first) & (pos < anchor)

    steps = s_ref.shape[0]
    whole = {0: steps // 2, steps // 2: steps - 1}.get(skip, steps) if small else steps
    for i in range(skip, steps):
        c = c0 + 2 * i
        low, high = slot(c, kv_ref.shape[0]), slot(c + 1, kv_ref.shape[0])
        k_t = jnp.concatenate([kv_ref[low, :, :hd], kv_ref[high, :, :hd]], axis=1)
        v = jnp.concatenate([kv_ref[low, :, hd:], kv_ref[high, :, hd:]], axis=0)
        z = dot(lhs_ref[...], k_t)
        s = z[:qr] * scale
        if i < whole:
            s = jnp.where(visible(c, (1, 2 * rows), 1), s, NEG)
        s_ref[i] = s
        m = jnp.maximum(s[:, :rows], s[:, rows:])
        if i > skip:
            m = jnp.maximum(max_ref[...], m)
        elif before is not None:
            m = jnp.maximum(before[0][...], m)
        max_ref[...] = m
        v = with_ones(v)
        if i < whole:
            v = v * jnp.where(visible(c, (2 * rows, 1), 0), 1.0, 0.0).astype(jnp.bfloat16)
        for h in range(heads):
            d = dot(softmaxes(z[qr + h * hd:qr + (h + 1) * hd], 0, small), v)
            if i > skip:
                d = state_ref[h] + d
            elif before is not None:
                d = before[1][h] + d
            state_ref[h] = d


def as_far_as_needed(first, anchor, rows, steps, most, run):
    small = most <= LIMIT
    pl.when(jnp.logical_not(small))(functools.partial(run, 0, False))
    left = small
    for skip in (steps - 1, steps // 2, 0):
        reached = first >= anchor - 4 * (steps - skip) * rows if skip else True
        pl.when(jnp.logical_and(left, reached))(functools.partial(run, skip, True))
        left = jnp.logical_and(left, jnp.logical_not(reached))


def same_core_kernel(at_ref, doc_ref, most_ref, a_ref, lhs_ref, s_ref, max_ref, state_ref):
    rows = max_ref.shape[1]
    chip, core = at_ref[0], at_ref[1]
    anchor = (2 * chip + core) * rows
    first = doc_start(doc_ref, anchor)
    steps = s_ref.shape[0]

    def run(skip, small):
        scan_keys(a_ref, lhs_ref, s_ref, max_ref, state_ref, chip - 2 * steps, core, first, anchor, None, skip, small)

    as_far_as_needed(first, anchor, rows, steps, jnp.max(most_ref[0:1, 0:1]), run)


def other_core_kernel(
    at_ref, doc_ref, most_ref, a_ref, b_ref, lhs_ref, sa_ref, max_a_ref, state_a_ref, sd_ref, peak_ref, phi_ref, nd_ref, v_own_ref,
    res_ref, loss_ref, sb_ref, max_ref, state_ref, acc_ref,
):
    heads, rows, hd = sd_ref.shape
    chip, core = at_ref[0], at_ref[1]
    anchor = (2 * chip + core) * rows
    first = doc_start(doc_ref, anchor)
    steps = sb_ref.shape[0]
    a0, b0 = chip - 2 * steps, chip - 2 * steps + core
    q_pos = anchor + lax.broadcasted_iota(jnp.int32, (rows, 1), 0)
    carried = jnp.broadcast_to(jnp.where(doc_start(doc_ref, q_pos) == first, 1.0, 0.0), (rows, hd)) > 0.5

    def run(skip, small):
        before = (max_a_ref, state_a_ref)
        scan_keys(b_ref, lhs_ref, sb_ref, max_ref, state_ref, b0, 1 - core, first, anchor, before, skip, small)
        for h in range(heads):
            at = slice(h * rows, (h + 1) * rows)
            off = jnp.broadcast_to(jnp.max(max_ref[at], axis=1, keepdims=True), (rows, hd))
            peak = jnp.maximum(peak_ref[h], jnp.where(carried, off, NEG))
            acc_ref[at] = dot(jnp.exp2(sd_ref[h] - peak).astype(jnp.bfloat16), v_own_ref[...])
            max_ref[at] = jnp.where(carried, peak, -NEG)

        weights, seen = [], []
        for kv_ref, s_ref, c0 in ((a_ref, sa_ref, a0), (b_ref, sb_ref, b0)):
            for i in range(skip, steps):
                c = c0 + 2 * i
                low, high = slot(c, kv_ref.shape[0]), slot(c + 1, kv_ref.shape[0])
                peak = max_ref[...]
                s = s_ref[i]
                weights.append(jnp.exp2(s[:, :rows] - peak).astype(jnp.bfloat16))
                weights.append(jnp.exp2(s[:, rows:] - peak).astype(jnp.bfloat16))
                seen.append(with_ones(kv_ref[low, :, hd:]))
                seen.append(with_ones(kv_ref[high, :, hd:]))
        acc_ref[...] += dot(jnp.concatenate(weights, axis=1), jnp.concatenate(seen, axis=0))

    as_far_as_needed(first, anchor, rows, steps, jnp.max(most_ref[0:1, 0:1]), run)

    squares = jnp.zeros((rows, hd), jnp.float32)
    for h in range(heads):
        acc = acc_ref[h * rows:(h + 1) * rows]
        state = state_ref[h]
        high = state.astype(jnp.bfloat16)
        low = (state - high.astype(jnp.float32)).astype(jnp.bfloat16)
        phi = phi_ref[h]
        nd = dot(phi, high) + dot(phi, low)
        own = nd_ref[h]
        numer = own[:, :hd] + jnp.where(carried, nd[:, :hd], 0.0)
        denom = own[:, hd:] + jnp.where(carried, nd[:, hd:], 0.0)
        residual = acc[:, :hd] / acc[:, hd:] - numer / denom
        res_ref[:, h * hd:(h + 1) * hd] = residual
        squares = squares + residual * residual
    loss = jnp.sum(jnp.transpose(squares), axis=0, keepdims=True) * (1.0 / hd)
    loss_ref[...] = jnp.broadcast_to(loss, loss_ref.shape)


F32, BF16 = jnp.float32, jnp.bfloat16
SMEM = pl.BlockSpec(memory_space=pltpu.SMEM)
VMEM = pl.BlockSpec(memory_space=pltpu.VMEM)


def rotated(array, axis, first):
    size = lax.axis_size(axis)
    group = [(first + j) % size for j in range(size)]
    return lax.all_to_all(array, axis, 0, 0, tiled=True, axis_index_groups=[group])


def shapes(*items):
    return tuple(jax.ShapeDtypeStruct(s, t) for s, t in items)


def params(mib):
    return pltpu.CompilerParams(vmem_limit_bytes=mib * 1024 * 1024)


def own_block(at, doc_lengths, queries, kv_own, fq_weight, fk_weight):
    rows = queries.shape[0]
    heads, hd, _ = fq_weight.shape
    return pl.pallas_call(
        own_kernel,
        out_shape=shapes(
            ((heads * (rows + hd), hd), BF16),
            ((heads, rows, rows), F32),
            ((heads, rows, rows), F32),
            ((heads, rows, 2 * hd), BF16),
            ((heads, rows, 2 * hd), F32),
            ((rows, 2 * hd), BF16),
            ((8, 128), F32),
        ),
        in_specs=[SMEM, SMEM] + [VMEM] * 4,
        out_specs=(VMEM,) * 7,
        compiler_params=params(16),
        cost_estimate=pl.CostEstimate(flops=10**9, bytes_accessed=2 * 10**6, transcendentals=10**6),
        name="own_block",
    )(at, doc_lengths, queries, kv_own, fq_weight, fk_weight)


def same_core(at, doc_lengths, most, a, lhs, heads):
    rows = hd = lhs.shape[1]
    steps = MAXDOC // (4 * rows)
    return pl.pallas_call(
        same_core_kernel,
        out_shape=shapes(
            ((steps, heads * rows, 2 * rows), F32), ((heads * rows, rows), F32), ((heads, 2 * hd, 2 * hd), F32)
        ),
        in_specs=[SMEM, SMEM, VMEM, VMEM, VMEM],
        out_specs=(VMEM,) * 3,
        compiler_params=params(16),
        cost_estimate=pl.CostEstimate(flops=2 * 10**9, bytes_accessed=4 * 10**6, transcendentals=2 * 10**6),
        name="same_core",
    )(at, doc_lengths, most, a, lhs)


def other_core(at, doc_lengths, most, a, b, lhs, sa, max_a, state_a, sd, peak, phi, nd, v_own, planes):
    heads, rows, hd = sd.shape
    return pl.pallas_call(
        other_core_kernel,
        out_shape=shapes(((rows, heads * hd), F32), ((planes, rows), F32)),
        in_specs=[SMEM] * 2 + [VMEM] * 12,
        out_specs=(VMEM, VMEM),
        scratch_shapes=[
            pltpu.VMEM(sa.shape, F32),
            pltpu.VMEM(max_a.shape, F32),
            pltpu.VMEM(state_a.shape, F32),
            pltpu.VMEM((heads * rows, 2 * hd), F32),
        ],
        compiler_params=params(24),
        cost_estimate=pl.CostEstimate(flops=4 * 10**9, bytes_accessed=4 * 10**6, transcendentals=4 * 10**6),
        name="other_core",
    )(at, doc_lengths, most, a, b, lhs, sa, max_a, state_a, sd, peak, phi, nd, v_own)


def body(queries, keys, values, doc_lengths, fq_weight, fk_weight):
    heads, hd, _ = fq_weight.shape
    at = jnp.stack([lax.axis_index(CHIP), lax.axis_index(CORE)]).astype(jnp.int32)
    kv_head = lax.axis_index("head") * (keys.shape[1] // hd) // lax.axis_size("head")
    k_own = lax.dynamic_slice_in_dim(keys, kv_head * hd, hd, 1)
    v_own = lax.dynamic_slice_in_dim(values, kv_head * hd, hd, 1)
    kv_own = jnp.concatenate([k_own.T, v_own], axis=1)
    send = jnp.broadcast_to(kv_own, (lax.axis_size(CHIP), *kv_own.shape))
    a = rotated(send, CHIP, FIRST_CHIP)
    lhs, sd, peak, phi, nd, v_own, most = own_block(at, doc_lengths, queries, kv_own, fq_weight, fk_weight)
    a, lhs = lax.optimization_barrier((a, lhs))
    b = lax.ppermute(a, CORE, [(0, 1), (1, 0)])
    sa, max_a, state_a = same_core(at, doc_lengths, most, a, lhs, heads)
    residual, loss = other_core(
        at, doc_lengths, most, a, b, lhs, sa, max_a, state_a, sd, peak, phi, nd, v_own, lax.axis_size("head")
    )
    parts = rotated(loss, "head", FIRST_PLANE)
    return residual, jnp.sum(parts, axis=0)


def solution(mesh):
    split = Mesh(mesh.devices.reshape(4, 4, 2, mesh.shape["head"]), (*SEQ, "head"))
    placed = (
        P(SEQ, "head"),
        P(SEQ, None),
        P(SEQ, None),
        P(),
        P("head", None, None),
        P("head", None, None),
    )
    return jax.shard_map(
        body, mesh=split, in_specs=placed, out_specs=(P(SEQ, "head"), P(SEQ)), check_vma=False
    )
```
